256 devices in a mesh: ctx: 32 (over y, z), head: 8 (over x, core).
Axes of the slice: x: 4, y: 4, z: 8, core: 2. Of those that a mesh axis runs over, the one named last changes fastest.
Arguments:
- query: bfloat16 [16384, 64, 128], P('ctx', 'head'), may hold values from -6 to 6
- key: bfloat16 [16384, 64, 128], P('ctx', 'head'), may hold values from -6 to 6
- value: bfloat16 [16384, 64, 128], P('ctx', 'head'), may hold values from -40 to 40
- gain: float32 [64, 128], P('head'), may hold values from 0.1 to 1.9
- cotangent: bfloat16 [16384, 64, 128], P('ctx', 'head'), may hold values from -6 to 6
- query2: bfloat16 [16384, 64, 128], P('ctx', 'head'), may hold values from -5 to 5
- key2: bfloat16 [16384, 8, 128], P('ctx', 'head'), may hold values from -5 to 5
- softmax_values: bfloat16 [16384, 8, 128], P('ctx', 'head'), may hold values from -6 to 6
Outputs:
- normed: bfloat16 [16384, 64, 128], P('ctx', 'head')
- grad_query: bfloat16 [16384, 64, 128], P('ctx', 'head')
- grad_key: bfloat16 [16384, 64, 128], P('ctx', 'head')
- grad_value: bfloat16 [16384, 64, 128], P('ctx', 'head')
- attended: bfloat16 [16384, 64, 128], P('ctx', 'head')
The draws below stay inside these ranges and needn't reach their ends.
All inputs are finite; a program needn't handle non-finite values.
Results may differ from the reference program's by a relative error of at most 0.02.
Values may be sent and summed in bfloat16 or wider, within the bound.
No kernel may reach another device: no remote copies, remote signals or barrier semaphores. Data moves between devices by JAX's collectives and lax.ppermute only.
A program may use at most 128 MiB of HBM per device.

```python
import math
import jax
import jax.numpy as jnp
from jax import lax

ATTN_HEADS = 64
HEAD_WIDTH = 128
KEY_VALUE_HEADS = 8
BLOCK_TOKENS = 512
WINDOW_BLOCKS = 4
SEQUENCE_TOKENS = 16384


def column_scales(key, heads):
    spread = jax.random.uniform(key, (heads, HEAD_WIDTH), jnp.float32)
    level = jnp.arange(heads, dtype=jnp.float32)[:, None] / max(heads - 1, 1)
    return jnp.exp(math.log(10.0) * (0.5 * level + 0.5 * spread))


def draw_value(key, part):
    key = jax.random.fold_in(key, 11)
    scale_key, base_key = jax.random.split(key, 2)
    scales = column_scales(scale_key, ATTN_HEADS)
    base_offset = jnp.clip(jax.random.normal(base_key, (SEQUENCE_TOKENS, ATTN_HEADS, HEAD_WIDTH), jnp.float32), -4.0, 4.0)
    return (scales[None] * base_offset).astype(jnp.bfloat16)


def draw_key2(key, part):
    key = jax.random.fold_in(key, 23)
    base_offset = jnp.clip(jax.random.normal(key, (SEQUENCE_TOKENS, KEY_VALUE_HEADS, HEAD_WIDTH), jnp.float32), -5.0, 5.0)
    return base_offset.astype(jnp.bfloat16)


def draw_query2(key, part):
    key = jax.random.fold_in(key, 37)
    scale_key, base_key = jax.random.split(key, 2)
    row_scale = jnp.exp(jax.random.uniform(scale_key, (SEQUENCE_TOKENS, 1, 1), jnp.float32, math.log(0.4), math.log(4.0)))
    base_offset = row_scale * jax.random.normal(base_key, (SEQUENCE_TOKENS, ATTN_HEADS, HEAD_WIDTH), jnp.float32)
    return jnp.clip(base_offset, -5.0, 5.0).astype(jnp.bfloat16)


def levels(rng, dims, cuts, low, top_value):
    def one(axis_at, parts):
        steps = jax.random.uniform(jax.random.fold_in(jax.random.fold_in(rng, 6), axis_at), (parts,), jnp.float32, low / len(cuts), top_value / len(cuts))
        return jnp.repeat(jnp.exp(steps), dims[axis_at] // parts).reshape((-1,) + (1,) * (len(dims) - axis_at - 1))

    level = one(*cuts[0])
    for cut in cuts[1:]:
        level = level * one(*cut)
    return level


def bell_draw(key, shape, scale, limit, cuts=(), held_as=jnp.bfloat16):
    values = scale * jax.random.normal(key, shape, jnp.float32)
    if cuts:
        values = values * levels(key, shape, cuts, -0.22, 0.18)
    return jnp.clip(values, -limit, limit).astype(held_as)


def setup_inputs(seed: int = 0) -> dict:
    seeds = jax.random.split(jax.random.key(seed), 9)
    return {
        "query": bell_draw(seeds[0], (SEQUENCE_TOKENS, ATTN_HEADS, HEAD_WIDTH), 1.0, 6.0, ((0, 32), (1, 8))),
        "key": bell_draw(seeds[1], (SEQUENCE_TOKENS, ATTN_HEADS, HEAD_WIDTH), 1.0, 6.0, ((0, 32), (1, 8))),
        "value": draw_value(jax.random.fold_in(seeds[8], 71), 0),
        "gain": jnp.clip(1.0 + 0.18 * jax.random.normal(seeds[3], (ATTN_HEADS, HEAD_WIDTH), jnp.float32), 0.1, 1.9),
        "cotangent": bell_draw(seeds[4], (SEQUENCE_TOKENS, ATTN_HEADS, HEAD_WIDTH), 1.0, 6.0, ((0, 32), (1, 8))),
        "query2": draw_query2(jax.random.fold_in(seeds[8], 71), 0),
        "key2": draw_key2(jax.random.fold_in(seeds[8], 71), 0),
        "softmax_values": bell_draw(seeds[7], (SEQUENCE_TOKENS, KEY_VALUE_HEADS, HEAD_WIDTH), 1.0, 6.0, ((0, 32), (1, 8))),
    }


epsilon = 1e-06
high = lax.Precision.HIGHEST

def round_half(values):
    rounded = values.astype(jnp.bfloat16)
    rounded = lax.optimization_barrier(rounded)
    return rounded.astype(jnp.float32)

def lower_mask(count):
    row_ids = lax.broadcasted_iota(jnp.int32, (count, count), 0)
    col_ids = lax.broadcasted_iota(jnp.int32, (count, count), 1)
    return col_ids <= row_ids

def split_heads(values):
    every_block = SEQUENCE_TOKENS // BLOCK_TOKENS
    return jnp.transpose(values.reshape(every_block, BLOCK_TOKENS, ATTN_HEADS, HEAD_WIDTH), (2, 0, 1, 3))

def merge_heads(values):
    return jnp.transpose(values, (1, 2, 0, 3)).reshape(SEQUENCE_TOKENS, ATTN_HEADS, HEAD_WIDTH)

def forward_head(inputs):
    query_h, key_h, value_h = inputs
    query_f = query_h.astype(jnp.float32)
    key_f = key_h.astype(jnp.float32)
    value_f = value_h.astype(jnp.float32)
    causal = lower_mask(BLOCK_TOKENS)[None]
    scores = jnp.einsum('bti,bsi->bts', query_f, key_f, precision=high)
    weights = round_half(jnp.where(causal, scores, 0.0))
    local = jnp.einsum('bts,bsj->btj', weights, value_f, precision=high)
    block_state = jnp.einsum('bsi,bsj->bij', key_f, value_f, precision=high)
    running = jnp.cumsum(block_state, axis=0)
    prefix = jnp.concatenate([jnp.zeros_like(block_state[:1]), running[:-1]], axis=0)
    attention = local + jnp.einsum('bti,bij->btj', query_f, prefix, precision=high)
    return (attention, prefix)

def backward_head(inputs):
    query_h, key_h, value_h, d_attention, prefix = inputs
    query_f = query_h.astype(jnp.float32)
    key_f = key_h.astype(jnp.float32)
    value_f = value_h.astype(jnp.float32)
    d_att = d_attention.astype(jnp.float32)
    causal = lower_mask(BLOCK_TOKENS)[None]
    scores = jnp.einsum('bti,bsi->bts', query_f, key_f, precision=high)
    weights = round_half(jnp.where(causal, scores, 0.0))
    d_scores = jnp.einsum('btj,bsj->bts', d_att, value_f, precision=high)
    d_weights = round_half(jnp.where(causal, d_scores, 0.0))
    grad_q = jnp.einsum('bts,bsi->bti', d_weights, key_f, precision=high)
    grad_q = grad_q + jnp.einsum('btj,bij->bti', d_att, prefix, precision=high)
    block_grad = jnp.einsum('bti,btj->bij', query_f, d_att, precision=high)
    running = jnp.cumsum(block_grad[::-1], axis=0)[::-1]
    suffix = jnp.concatenate([running[1:], jnp.zeros_like(block_grad[:1])], axis=0)
    grad_k = jnp.einsum('bts,bti->bsi', d_weights, query_f, precision=high)
    grad_k = grad_k + jnp.einsum('bsj,bij->bsi', value_f, suffix, precision=high)
    grad_v = jnp.einsum('bts,btj->bsj', weights, d_att, precision=high)
    grad_v = grad_v + jnp.einsum('bsi,bij->bsj', key_f, suffix, precision=high)
    return (grad_q.astype(jnp.bfloat16), grad_k.astype(jnp.bfloat16), grad_v.astype(jnp.bfloat16))

def window_attention(query2, key2, softmax_values):
    query_group_count = ATTN_HEADS // KEY_VALUE_HEADS
    every_block = SEQUENCE_TOKENS // BLOCK_TOKENS
    padding_width = jnp.zeros(((WINDOW_BLOCKS - 1) * BLOCK_TOKENS, KEY_VALUE_HEADS, HEAD_WIDTH), jnp.float32)
    key_pad = jnp.concatenate([padding_width, key2.astype(jnp.float32)], axis=0)
    value_pad = jnp.concatenate([padding_width, softmax_values.astype(jnp.float32)], axis=0)

    def one_block(block):
        begin = (block * BLOCK_TOKENS).astype(jnp.int32)
        query_block = lax.dynamic_slice_in_dim(query2, begin, BLOCK_TOKENS, 0).astype(jnp.float32)
        query_block = query_block.reshape(BLOCK_TOKENS, KEY_VALUE_HEADS, query_group_count, HEAD_WIDTH)
        key_b = lax.dynamic_slice_in_dim(key_pad, begin, WINDOW_BLOCKS * BLOCK_TOKENS, 0)
        value_b = lax.dynamic_slice_in_dim(value_pad, begin, WINDOW_BLOCKS * BLOCK_TOKENS, 0)
        logits = jnp.einsum('tkgd,skd->kgts', query_block, key_b, precision=high) * HEAD_WIDTH ** (-0.5)
        key_pos = begin - (WINDOW_BLOCKS - 1) * BLOCK_TOKENS + jnp.arange(WINDOW_BLOCKS * BLOCK_TOKENS, dtype=jnp.int32)
        query_pos = begin + jnp.arange(BLOCK_TOKENS, dtype=jnp.int32)
        usable = (key_pos[None, :] >= 0) & (key_pos[None, :] <= query_pos[:, None])
        logits = jnp.where(usable, logits, -1e+30)
        row_max = lax.optimization_barrier(jnp.max(logits, axis=-1, keepdims=True))
        exponent = jnp.exp(logits - row_max)
        probs = round_half(exponent / lax.optimization_barrier(jnp.sum(exponent, axis=-1, keepdims=True)))
        result = jnp.einsum('kgts,skd->tkgd', probs, value_b, precision=high)
        return result.reshape(BLOCK_TOKENS, ATTN_HEADS, HEAD_WIDTH).astype(jnp.bfloat16)
    results = lax.map(one_block, jnp.arange(every_block, dtype=jnp.int32))
    return results.reshape(SEQUENCE_TOKENS, ATTN_HEADS, HEAD_WIDTH)

def reference(query, key, value, gain, cotangent, query2, key2, softmax_values):
    query_h = split_heads(query)
    key_h = split_heads(key)
    value_h = split_heads(value)
    attention, prefix = lax.map(forward_head, (query_h, key_h, value_h))
    total_sq = lax.optimization_barrier(jnp.sum(attention * attention, axis=(0, 3)))
    inverse_rms = 1.0 / jnp.sqrt(total_sq / (ATTN_HEADS * HEAD_WIDTH) + epsilon)
    unit = attention * inverse_rms[None, :, :, None]
    gain_b = gain[:, None, None, :]
    normed = merge_heads((gain_b * unit).astype(jnp.bfloat16))
    grad_in = gain_b * split_heads(cotangent).astype(jnp.float32)
    mean_grad = lax.optimization_barrier(jnp.sum(unit * grad_in, axis=(0, 3))) / (ATTN_HEADS * HEAD_WIDTH)
    d_attention = ((grad_in - unit * mean_grad[None, :, :, None]) * inverse_rms[None, :, :, None]).astype(jnp.bfloat16)
    grad_q, grad_k, grad_v = lax.map(backward_head, (query_h, key_h, value_h, d_attention, prefix))
    softmax_query = (query2.astype(jnp.float32) + normed.astype(jnp.float32)).astype(jnp.bfloat16)
    attended = window_attention(softmax_query, key2, softmax_values)
    return (normed, merge_heads(grad_q), merge_heads(grad_k), merge_heads(grad_v), attended)
```

```python
import functools
import jax
import jax.numpy as jnp
from jax import lax
from jax.experimental import pallas as pl
from jax.experimental.pallas import tpu as pltpu
from jax.sharding import Mesh, PartitionSpec as P

ATTN_HEADS = 64
HEAD_WIDTH = 128
WINDOW_BLOCKS = 4
CHANNELS = ATTN_HEADS * HEAD_WIDTH
EPSILON = 1e-06
LOG2E = 1.4426950408889634

f32 = jnp.float32
bf16 = jnp.bfloat16
MIB = 1 << 20
HEADS = ("x", "core")
CTX = ("y", "z")


def nn(a, b, precision=None):
    return lax.dot_general(
        a, b, (((1,), (0,)), ((), ())), precision=precision, preferred_element_type=f32
    )


def nt(a, b, precision=None):
    return lax.dot_general(
        a, b, (((1,), (1,)), ((), ())), precision=precision, preferred_element_type=f32
    )


def tn(a, b, precision=None):
    return lax.dot_general(
        a, b, (((0,), (0,)), ((), ())), precision=precision, preferred_element_type=f32
    )


def call(kernel, out_shapes, args, scratch=(), flops=0, smem_first=False, vmem=48):
    specs = [pl.BlockSpec(memory_space=pltpu.VMEM) for _ in args]
    if smem_first:
        specs[0] = pl.BlockSpec(memory_space=pltpu.SMEM)
    moved = sum(a.size * a.dtype.itemsize for a in (*args, *out_shapes))
    return pl.pallas_call(
        kernel,
        out_shape=out_shapes,
        in_specs=specs,
        out_specs=[pl.BlockSpec(memory_space=pltpu.VMEM) for _ in out_shapes],
        scratch_shapes=list(scratch),
        compiler_params=pltpu.CompilerParams(vmem_limit_bytes=vmem * MIB),
        cost_estimate=pl.CostEstimate(flops=flops, bytes_accessed=moved, transcendentals=0),
    )(*args)


def shape(dims, dtype):
    return jax.ShapeDtypeStruct(dims, dtype)


def state_kernel(k_ref, v_ref, kh_ref, vh_ref, st_ref, ks, vs):
    tokens, heads, width = k_ref.shape
    ks[...] = k_ref[...].astype(f32).reshape(tokens * heads, width)
    vs[...] = v_ref[...].astype(f32).reshape(tokens * heads, width)
    for h in range(heads):
        kh = ks[pl.ds(h, tokens, stride=heads), :].astype(bf16)
        vh = vs[pl.ds(h, tokens, stride=heads), :].astype(bf16)
        kh_ref[h] = kh
        vh_ref[h] = vh
        st_ref[h] = tn(kh, vh).astype(bf16)


def causal_below(rows):
    r = lax.broadcasted_iota(jnp.int32, (rows, rows), 0)
    c = lax.broadcasted_iota(jnp.int32, (rows, rows), 1)
    return c <= r


def local_kernel(q_ref, c_ref, gain_ref, kh_ref, vh_ref, qh_ref, gh_ref, loc_ref, qs, cs):
    tokens, heads, width = q_ref.shape
    half = tokens // 2
    qs[...] = q_ref[...].astype(f32).reshape(tokens * heads, width)
    cs[...] = (c_ref[...].astype(f32) * gain_ref[...][None]).reshape(tokens * heads, width)
    causal = causal_below(half)
    for h in range(heads):
        qh = qs[pl.ds(h, tokens, stride=heads), :].astype(bf16)
        qh_ref[h] = qh
        gh_ref[h] = cs[pl.ds(h, tokens, stride=heads), :]
        kh = kh_ref[h]
        vh = vh_ref[h]
        w0 = jnp.where(causal, nt(qh[:half], kh[:half]), 0.0).astype(bf16)
        w10 = nt(qh[half:], kh[:half]).astype(bf16)
        w11 = jnp.where(causal, nt(qh[half:], kh[half:]), 0.0).astype(bf16)
        loc_ref[h, :half] = nn(w0, vh[:half])
        loc_ref[h, half:] = nn(w10, vh[:half]) + nn(w11, vh[half:])


def attention_kernel(loc_ref, qh_ref, gh_ref, pre_ref, att_ref, part_ref):
    heads, tokens, width = loc_ref.shape
    squares = jnp.zeros((tokens, width), f32)
    inner = jnp.zeros((tokens, width), f32)
    for h in range(heads):
        att = loc_ref[h] + nn(qh_ref[h], pre_ref[h])
        att_ref[h] = att
        squares = squares + att * att
        inner = inner + att * gh_ref[h]
    ones = jnp.ones((8, width), f32)
    part_ref[0:1] = nt(ones, squares, lax.Precision.HIGHEST)[0:1]
    part_ref[1:2] = nt(ones, inner, lax.Precision.HIGHEST)[0:1]


def row_scales(g_ref):
    ones = jnp.ones((g_ref.shape[0], HEAD_WIDTH), f32)
    squares = tn(g_ref[:, 0, :], ones, lax.Precision.HIGHEST)
    inner = tn(g_ref[:, 1, :], ones, lax.Precision.HIGHEST)
    inverse = 1.0 / jnp.sqrt(squares / CHANNELS + EPSILON)
    return inverse, inverse * inner / CHANNELS


def backward_kernel(g_ref, att_ref, gh_ref, qh_ref, da_ref, bg_ref, inv_ref):
    heads, tokens, width = att_ref.shape
    inverse, mean = row_scales(g_ref)
    inv_ref[...] = inverse
    scaled = inverse * mean
    for h in range(heads):
        da = ((gh_ref[h] - att_ref[h] * scaled) * inverse).astype(bf16)
        da_ref[h] = da
        bg_ref[h] = tn(qh_ref[h], da).astype(bf16)


def softmax_kernel(
    pos_ref, att_ref, inv_ref, gain_ref, q2_ref, kv0_ref, kv1_ref, kv2_ref, kv3_ref,
    norm_ref, out_ref, scratch,
):
    heads, tokens, width = att_ref.shape
    inverse = inv_ref[...]
    for h in range(heads):
        scratch[pl.ds(h, tokens, stride=heads), :] = (
            gain_ref[h : h + 1, :] * (att_ref[h] * inverse)
        )
    normed = scratch[...].astype(bf16)
    norm_ref[...] = normed.reshape(tokens, heads, width)

    rows = 256
    groups = 4
    chunks = tokens * heads // rows
    per_group = chunks // groups
    scale = LOG2E * HEAD_WIDTH ** (-0.5)
    ones = jnp.ones((tokens, width), bf16)
    token_chunk = rows // heads
    blocks = (kv0_ref, kv1_ref, kv2_ref, kv3_ref)

    def run(count):
        for group in range(groups):
            limit = tokens // groups * (group + 1)

            def body(step, carry):
                chunk = group * per_group + step
                first = pl.multiple_of(chunk * rows, rows)
                t0 = pl.multiple_of(chunk * token_chunk, token_chunk)
                n = scratch[pl.ds(first, rows), :].astype(bf16).astype(f32)
                q2 = q2_ref[pl.ds(t0, token_chunk)].astype(f32).reshape(rows, width)
                q = (q2 + n).astype(bf16)
                row_token = t0 + lax.broadcasted_iota(jnp.int32, (rows, limit), 0) // heads
                column = lax.broadcasted_iota(jnp.int32, (rows, limit), 1)
                scores = [
                    jnp.where(column <= row_token, nt(q, blocks[0][0, :limit]), -1e30)
                ]
                for b in range(1, count):
                    scores.append(nt(q, blocks[b][0]))
                top = jnp.max(scores[0], axis=1, keepdims=True)
                for s in scores[1:]:
                    top = jnp.maximum(top, jnp.max(s, axis=1, keepdims=True))
                top = top * scale
                total = None
                for b, s in enumerate(scores):
                    p = jnp.exp2(s * scale - top).astype(bf16)
                    n_keys = s.shape[1]
                    v = jnp.concatenate([blocks[b][1, :n_keys], ones[:n_keys]], axis=1)
                    o = nn(p, v)
                    total = o if total is None else total + o
                result = total[:, :width] / total[:, width:]
                out_ref[pl.ds(t0, token_chunk)] = result.astype(bf16).reshape(
                    token_chunk, heads, width
                )
                return carry

            lax.fori_loop(0, per_group, body, 0)

    have = pos_ref[0]
    for count in range(1, WINDOW_BLOCKS + 1):
        pl.when(have == count - 1)(functools.partial(run, count))


def gradient_kernel(
    qh_ref, kh_ref, vh_ref, da_ref, pre_ref, suf_ref, gq_ref, gk_ref, gv_ref, qs, ks, vs
):
    heads, tokens, width = qh_ref.shape
    half = tokens // 2
    below = causal_below(half)
    r = lax.broadcasted_iota(jnp.int32, (half, half), 0)
    c = lax.broadcasted_iota(jnp.int32, (half, half), 1)
    above = r <= c
    lo, hi = slice(0, half), slice(half, tokens)

    def low(x):
        return jnp.where(below, x, 0.0).astype(bf16)

    def up(x):
        return jnp.where(above, x, 0.0).astype(bf16)

    for h in range(heads):
        q, k, v, da = qh_ref[h], kh_ref[h], vh_ref[h], da_ref[h]
        pre, suf = pre_ref[h], suf_ref[h]
        d00 = low(nt(da[lo], v[lo]))
        d10 = nt(da[hi], v[lo]).astype(bf16)
        d11 = low(nt(da[hi], v[hi]))
        gq = nt(da, pre)
        gq0 = gq[lo] + nn(d00, k[lo])
        gq1 = gq[hi] + nn(d10, k[lo]) + nn(d11, k[hi])
        t00 = up(nt(v[lo], da[lo]))
        t01 = nt(v[lo], da[hi]).astype(bf16)
        t11 = up(nt(v[hi], da[hi]))
        gk = nt(v, suf)
        gk0 = gk[lo] + nn(t00, q[lo]) + nn(t01, q[hi])
        gk1 = gk[hi] + nn(t11, q[hi])
        w00 = up(nt(k[lo], q[lo]))
        w01 = nt(k[lo], q[hi]).astype(bf16)
        w11 = up(nt(k[hi], q[hi]))
        gv = nn(k, suf)
        gv0 = gv[lo] + nn(w00, da[lo]) + nn(w01, da[hi])
        gv1 = gv[hi] + nn(w11, da[hi])
        for ref, first, second in ((qs, gq0, gq1), (ks, gk0, gk1), (vs, gv0, gv1)):
            ref[pl.ds(h, half, stride=heads), :] = first
            ref[pl.ds(half * heads + h, half, stride=heads), :] = second
    for ref, out in ((qs, gq_ref), (ks, gk_ref), (vs, gv_ref)):
        out[...] = ref[...].astype(bf16).reshape(tokens, heads, width)


def scan_kernel(back, recv_ref, t1_ref, t2_ref, t3_ref, out_ref):
    count = recv_ref.shape[0]
    running = t1_ref[...].astype(f32) + t2_ref[...].astype(f32) + t3_ref[...].astype(f32)
    order = range(count - 1, -1, -1) if back else range(count)
    for i in order:
        out_ref[i] = running.astype(bf16)
        running = running + recv_ref[i].astype(f32)


def total_kernel(recv_ref, out_ref):
    total = recv_ref[0].astype(f32)
    for i in range(1, recv_ref.shape[0]):
        total = total + recv_ref[i].astype(f32)
    out_ref[...] = total.astype(bf16)


def exclusive(states, back):
    pieces = lax.all_to_all(states, "z", 0, 0, tiled=True)
    (total,) = call(total_kernel, [shape(states.shape[1:], bf16)], [pieces])
    rows = lax.axis_size("y")
    others = []
    for d in range(1, 4):
        pairs = [(i + d, i) if back else (i, i + d) for i in range(rows - d)]
        others.append(lax.ppermute(total, "y", pairs))
    (scanned,) = call(
        functools.partial(scan_kernel, back), [shape(pieces.shape, bf16)], [pieces, *others]
    )
    return lax.all_to_all(scanned, "z", 0, 0, tiled=True)


def local(query, key, value, gain, cotangent, query2, key2, softmax_values):
    tokens, heads, width = query.shape
    position = lax.axis_index(CTX)
    flat = (tokens * heads, width)
    head_major = (heads, tokens, width)
    square = (heads, width, width)
    unit = 2 * tokens * tokens * width * heads

    own = jnp.stack((key2[:, 0], softmax_values[:, 0]))
    ring = lax.axis_size(CTX)
    windows = [own]
    for _ in range(1, WINDOW_BLOCKS):
        windows.append(
            lax.ppermute(windows[-1], CTX, [(i, i + 1) for i in range(ring - 1)])
        )

    kh, vh, states = call(
        state_kernel,
        [shape(head_major, bf16), shape(head_major, bf16), shape(square, bf16)],
        [key, value],
        [pltpu.VMEM(flat, f32), pltpu.VMEM(flat, f32)],
        unit // 4,
    )
    prefix = exclusive(states, False)
    qh, gh, loc = call(
        local_kernel,
        [shape(head_major, bf16), shape(head_major, f32), shape(head_major, f32)],
        [query, cotangent, gain, kh, vh],
        [pltpu.VMEM(flat, f32), pltpu.VMEM(flat, f32)],
        2 * unit,
    )
    att, part = call(
        attention_kernel,
        [shape(head_major, f32), shape((2, tokens), f32)],
        [loc, qh, gh, prefix],
        (),
        unit // 4,
    )
    gathered = lax.all_gather(part, HEADS)
    da, block_grad, inverse = call(
        backward_kernel,
        [shape(head_major, bf16), shape(square, bf16), shape((tokens, width), f32)],
        [gathered, att, gh, qh],
        (),
        unit // 4,
    )
    suffix = exclusive(block_grad, True)
    have = jnp.minimum(position, WINDOW_BLOCKS - 1).astype(jnp.int32).reshape(1)
    normed, attended = call(
        softmax_kernel,
        [shape(query.shape, bf16), shape(query.shape, bf16)],
        [have, att, inverse, gain, query2, *windows],
        [pltpu.VMEM(flat, f32)],
        8 * unit,
        smem_first=True,
    )
    gq, gk, gv = call(
        gradient_kernel,
        [shape(query.shape, bf16)] * 3,
        [qh, kh, vh, da, prefix, suffix],
        [pltpu.VMEM(flat, f32)] * 3,
        6 * unit,
    )
    return normed, gq, gk, gv, attended


def solution(mesh):
    sizes = (4, 8, 4, 2)
    fine = Mesh(mesh.devices.reshape(sizes), ("y", "z", "x", "core"))
    tokens = P(CTX, HEADS, None)
    return jax.shard_map(
        local,
        mesh=fine,
        in_specs=(tokens, tokens, tokens, P(HEADS, None), tokens, tokens, tokens, tokens),
        out_specs=(tokens,) * 5,
        check_vma=False,
    )
```

```python
import functools
import jax
import jax.numpy as jnp
from jax import lax
from jax.experimental import pallas as pl
from jax.experimental.pallas import tpu as pltpu
from jax.sharding import Mesh, PartitionSpec as P

ATTN_HEADS = 64
HEAD_WIDTH = 128
WINDOW_BLOCKS = 4
CHANNELS = ATTN_HEADS * HEAD_WIDTH
EPSILON = 1e-06
LOG2E = 1.4426950408889634

f32 = jnp.float32
bf16 = jnp.bfloat16
MIB = 1 << 20
HEADS = ("x", "core")
CTX = ("y", "z")


def nn(a, b, precision=None):
    return lax.dot_general(
        a, b, (((1,), (0,)), ((), ())), precision=precision, preferred_element_type=f32
    )


def nt(a, b, precision=None):
    return lax.dot_general(
        a, b, (((1,), (1,)), ((), ())), precision=precision, preferred_element_type=f32
    )


def tn(a, b, precision=None):
    return lax.dot_general(
        a, b, (((0,), (0,)), ((), ())), precision=precision, preferred_element_type=f32
    )


def call(kernel, out_shapes, args, scratch=(), flops=0, smem_first=False, vmem=20, hbm_in=(), hbm_out=()):
    def place(i, far):
        return pl.BlockSpec(memory_space=pltpu.HBM if i in far else pltpu.VMEM)

    specs = [place(i, hbm_in) for i in range(len(args))]
    if smem_first:
        specs[0] = pl.BlockSpec(memory_space=pltpu.SMEM)
    moved = sum(a.size * a.dtype.itemsize for a in (*args, *out_shapes))
    return pl.pallas_call(
        kernel,
        out_shape=out_shapes,
        in_specs=specs,
        out_specs=[place(i, hbm_out) for i in range(len(out_shapes))],
        scratch_shapes=list(scratch),
        compiler_params=pltpu.CompilerParams(vmem_limit_bytes=vmem * MIB),
        cost_estimate=pl.CostEstimate(flops=flops, bytes_accessed=moved, transcendentals=0),
    )(*args)


def shape(dims, dtype):
    return jax.ShapeDtypeStruct(dims, dtype)


def state_kernel(k_ref, v_ref, kh_ref, vh_ref, st_ref, kb, vb, ks, vs, sems):
    tokens, heads, width = k_ref.shape
    pieces = sems.shape[1]
    rows = tokens // pieces
    copies = []
    for i in range(pieces):
        part = pl.ds(i * rows, rows)
        for j, (src, dst) in enumerate(((k_ref, kb), (v_ref, vb))):
            copy = pltpu.make_async_copy(src.at[part], dst.at[part], sems.at[j, i])
            copy.start()
            copies.append((copy, dst, (ks, vs)[j], i))
    for copy, buffer, flat, i in copies:
        copy.wait()
        flat[pl.ds(i * rows * heads, rows * heads), :] = (
            buffer[pl.ds(i * rows, rows)].astype(f32).reshape(rows * heads, width)
        )
    for h in range(heads):
        kh = ks[pl.ds(h, tokens, stride=heads), :].astype(bf16)
        vh = vs[pl.ds(h, tokens, stride=heads), :].astype(bf16)
        kh_ref[h] = kh
        vh_ref[h] = vh
        st_ref[h] = tn(kh, vh).astype(bf16)


def causal_below(rows):
    r = lax.broadcasted_iota(jnp.int32, (rows, rows), 0)
    c = lax.broadcasted_iota(jnp.int32, (rows, rows), 1)
    return c <= r


def local_kernel(q_ref, c_ref, gain_ref, kh_ref, vh_ref, qh_ref, gh_ref, loc_ref, qs, cs):
    tokens, heads, width = q_ref.shape
    half = tokens // 2
    qs[...] = q_ref[...].astype(f32).reshape(tokens * heads, width)
    cs[...] = (c_ref[...].astype(f32) * gain_ref[...][None]).reshape(tokens * heads, width)
    causal = causal_below(half)
    for h in range(heads):
        qh = qs[pl.ds(h, tokens, stride=heads), :].astype(bf16)
        qh_ref[h] = qh
        gh_ref[h] = cs[pl.ds(h, tokens, stride=heads), :]
        kh = kh_ref[h]
        vh = vh_ref[h]
        w0 = jnp.where(causal, nt(qh[:half], kh[:half]), 0.0).astype(bf16)
        w10 = nt(qh[half:], kh[:half]).astype(bf16)
        w11 = jnp.where(causal, nt(qh[half:], kh[half:]), 0.0).astype(bf16)
        loc_ref[h, :half] = nn(w0, vh[:half])
        loc_ref[h, half:] = nn(w10, vh[:half]) + nn(w11, vh[half:])


def attention_kernel(loc_ref, qh_ref, gh_ref, pre_ref, att_ref, part_ref):
    heads, tokens, width = loc_ref.shape
    squares = jnp.zeros((tokens, width), f32)
    inner = jnp.zeros((tokens, width), f32)
    for h in range(heads):
        att = loc_ref[h] + nn(qh_ref[h], pre_ref[h])
        att_ref[h] = att
        squares = squares + att * att
        inner = inner + att * gh_ref[h]
    ones = jnp.ones((8, width), f32)
    rows = jnp.concatenate(
        [
            nt(ones, squares, lax.Precision.HIGHEST)[0:1],
            nt(ones, inner, lax.Precision.HIGHEST)[0:1],
        ]
    )
    for j in range(part_ref.shape[0]):
        part_ref[j] = rows


def row_scales(g_ref):
    ones = jnp.ones((g_ref.shape[0], HEAD_WIDTH), f32)
    squares = tn(g_ref[:, 0, :], ones, lax.Precision.HIGHEST)
    inner = tn(g_ref[:, 1, :], ones, lax.Precision.HIGHEST)
    inverse = 1.0 / jnp.sqrt(squares / CHANNELS + EPSILON)
    return inverse, inverse * inner / CHANNELS


def backward_kernel(g_ref, att_ref, gh_ref, qh_ref, da_ref, bg_ref, inv_ref):
    heads, tokens, width = att_ref.shape
    inverse, mean = row_scales(g_ref)
    inv_ref[...] = inverse
    scaled = inverse * mean
    for h in range(heads):
        da = ((gh_ref[h] - att_ref[h] * scaled) * inverse).astype(bf16)
        da_ref[h] = da
        bg_ref[h] = tn(qh_ref[h], da).astype(bf16)


def softmax_kernel(
    pos_ref, att_ref, inv_ref, gain_ref, q2_ref, kv0_ref, kv1_ref, kv2_ref, kv3_ref,
    norm_ref, out_ref, scratch,
):
    heads, tokens, width = att_ref.shape
    inverse = inv_ref[...]
    for h in range(heads):
        scratch[pl.ds(h, tokens, stride=heads), :] = (
            gain_ref[h : h + 1, :] * (att_ref[h] * inverse)
        )
    normed = scratch[...].astype(bf16)
    norm_ref[...] = normed.reshape(tokens, heads, width)

    rows = 256
    groups = 4
    chunks = tokens * heads // rows
    per_group = chunks // groups
    scale = LOG2E * HEAD_WIDTH ** (-0.5)
    ones = jnp.ones((tokens, width), bf16)
    token_chunk = rows // heads
    blocks = (kv0_ref, kv1_ref, kv2_ref, kv3_ref)

    def run(count):
        for group in range(groups):
            limit = tokens // groups * (group + 1)

            def body(step, carry):
                chunk = group * per_group + step
                first = pl.multiple_of(chunk * rows, rows)
                t0 = pl.multiple_of(chunk * token_chunk, token_chunk)
                n = scratch[pl.ds(first, rows), :].astype(bf16).astype(f32)
                q2 = q2_ref[pl.ds(t0, token_chunk)].astype(f32).reshape(rows, width)
                q = (q2 + n).astype(bf16)
                row_token = t0 + lax.broadcasted_iota(jnp.int32, (rows, limit), 0) // heads
                column = lax.broadcasted_iota(jnp.int32, (rows, limit), 1)
                scores = [
                    jnp.where(column <= row_token, nt(q, blocks[0][0, :limit]), -1e30)
                ]
                for b in range(1, count):
                    scores.append(nt(q, blocks[b][0]))
                top = jnp.max(scores[0], axis=1, keepdims=True)
                for s in scores[1:]:
                    top = jnp.maximum(top, jnp.max(s, axis=1, keepdims=True))
                top = top * scale
                total = None
                for b, s in enumerate(scores):
                    p = jnp.exp2(s * scale - top).astype(bf16)
                    n_keys = s.shape[1]
                    v = jnp.concatenate([blocks[b][1, :n_keys], ones[:n_keys]], axis=1)
                    o = nn(p, v)
                    total = o if total is None else total + o
                result = total[:, :width] / total[:, width:]
                out_ref[pl.ds(t0, token_chunk)] = result.astype(bf16).reshape(
                    token_chunk, heads, width
                )
                return carry

            lax.fori_loop(0, per_group, body, 0, unroll=4 if count > 2 else 2)

    have = pos_ref[0]
    for count in range(1, WINDOW_BLOCKS + 1):
        pl.when(have == count - 1)(functools.partial(run, count))


def query_gradient_kernel(kh_ref, vh_ref, da_ref, pre_ref, gq_ref, qs):
    heads, tokens, width = kh_ref.shape
    half = tokens // 2
    below = causal_below(half)
    lo, hi = slice(0, half), slice(half, tokens)
    for h in range(heads):
        k, v, da = kh_ref[h], vh_ref[h], da_ref[h]
        d00 = jnp.where(below, nt(da[lo], v[lo]), 0.0).astype(bf16)
        d10 = nt(da[hi], v[lo]).astype(bf16)
        d11 = jnp.where(below, nt(da[hi], v[hi]), 0.0).astype(bf16)
        gq = nt(da, pre_ref[h])
        qs[pl.ds(h, half, stride=heads), :] = gq[lo] + nn(d00, k[lo])
        qs[pl.ds(half * heads + h, half, stride=heads), :] = (
            gq[hi] + nn(d10, k[lo]) + nn(d11, k[hi])
        )
    gq_ref[...] = qs[...].astype(bf16).reshape(tokens, heads, width)


def key_value_local_kernel(qh_ref, kh_ref, vh_ref, da_ref, gk_ref, gv_ref):
    heads, tokens, width = qh_ref.shape
    half = tokens // 2
    r = lax.broadcasted_iota(jnp.int32, (half, half), 0)
    c = lax.broadcasted_iota(jnp.int32, (half, half), 1)
    above = r <= c
    lo, hi = slice(0, half), slice(half, tokens)

    def up(x):
        return jnp.where(above, x, 0.0).astype(bf16)

    for h in range(heads):
        q, k, v, da = qh_ref[h], kh_ref[h], vh_ref[h], da_ref[h]
        for out, a, b, other in ((gk_ref, v, da, q), (gv_ref, k, q, da)):
            m00 = up(nt(a[lo], b[lo]))
            m01 = nt(a[lo], b[hi]).astype(bf16)
            m11 = up(nt(a[hi], b[hi]))
            out[h, :half] = nn(m00, other[lo]) + nn(m01, other[hi])
            out[h, half:] = nn(m11, other[hi])


def finish_kernel(kh_ref, vh_ref, pk_ref, pv_ref, suf_ref, gk_ref, gv_ref, ks, vs, kb, vb, sems):
    heads, tokens, width = kh_ref.shape
    pieces = sems.shape[1]
    rows = tokens // pieces
    copies = []
    for i in range(pieces):
        part = pl.ds(i * rows, rows)
        for h in range(heads):
            suf = suf_ref[h]
            target = pl.ds(i * rows * heads + h, rows, stride=heads)
            ks[target, :] = pk_ref[h, part] + nt(vh_ref[h, part], suf)
            vs[target, :] = pv_ref[h, part] + nn(kh_ref[h, part], suf)
        flat = pl.ds(i * rows * heads, rows * heads)
        for j, (src, buffer, out) in enumerate(((ks, kb, gk_ref), (vs, vb, gv_ref))):
            buffer[part] = src[flat, :].astype(bf16).reshape(rows, heads, width)
            copy = pltpu.make_async_copy(buffer.at[part], out.at[part], sems.at[j, i])
            copy.start()
            copies.append(copy)
    for copy in copies:
        copy.wait()


def scan_kernel(back, pos_ref, recv_ref, totals_ref, out_ref):
    count = recv_ref.shape[0]
    row = pos_ref[0]
    running = jnp.zeros(totals_ref.shape[1:], f32)
    for j in range(totals_ref.shape[0]):
        counts = (j > row) if back else (j < row)
        running = running + jnp.where(counts, totals_ref[j].astype(f32), 0.0)
    order = range(count - 1, -1, -1) if back else range(count)
    for i in order:
        out_ref[i] = running.astype(bf16)
        running = running + recv_ref[i].astype(f32)


def total_kernel(recv_ref, out_ref):
    total = recv_ref[0].astype(f32)
    for i in range(1, recv_ref.shape[0]):
        total = total + recv_ref[i].astype(f32)
    for j in range(out_ref.shape[0]):
        out_ref[j] = total.astype(bf16)


def tied(first, second):
    return lax.optimization_barrier((first, second))


def row_totals(pieces):
    rows = lax.axis_size("y")
    (totals,) = call(total_kernel, [shape((rows, *pieces.shape[1:]), bf16)], [pieces])
    return lax.all_to_all(totals, "y", 0, 0, tiled=True)


def scanned(pieces, totals, back):
    row = lax.axis_index("y").astype(jnp.int32).reshape(1)
    return call(
        functools.partial(scan_kernel, back),
        [shape(pieces.shape, bf16)],
        [row, pieces, totals],
        smem_first=True,
    )[0]


def spread(x):
    return lax.all_to_all(x, "z", 0, 0, tiled=True)


def local(query, key, value, gain, cotangent, query2, key2, softmax_values):
    tokens, heads, width = query.shape
    position = lax.axis_index(CTX)
    flat = (tokens * heads, width)
    head_major = (heads, tokens, width)
    square = (heads, width, width)
    unit = 2 * tokens * tokens * width * heads
    ring = lax.axis_size(CTX)
    members = lax.axis_size(HEADS)
    token_buffer = pltpu.VMEM(query.shape, bf16)
    flat_buffer = pltpu.VMEM(flat, f32)
    copy_sems = pltpu.SemaphoreType.DMA((2, 4))

    def onward(x):
        return lax.ppermute(x, CTX, [(i, i + 1) for i in range(ring - 1)])

    kv0 = jnp.stack((key2[:, 0], softmax_values[:, 0]))
    kv1 = onward(kv0)

    kh, vh, states = call(
        state_kernel,
        [shape(head_major, bf16), shape(head_major, bf16), shape(square, bf16)],
        [key, value],
        [token_buffer, token_buffer, flat_buffer, flat_buffer, copy_sems],
        unit // 4,
        hbm_in=(0, 1),
    )
    pieces = spread(states)
    qh, gh, loc = call(
        local_kernel,
        [shape(head_major, bf16), shape(head_major, f32), shape(head_major, f32)],
        [query, cotangent, gain, kh, vh],
        [flat_buffer, flat_buffer],
        2 * unit,
    )
    pieces, kv1 = tied(pieces, kv1)
    kv2 = onward(kv1)
    totals, kv2 = tied(row_totals(pieces), kv2)
    prefix, kv2 = tied(spread(scanned(pieces, totals, False)), kv2)
    kv3 = onward(kv2)
    att, part = call(
        attention_kernel,
        [shape(head_major, f32), shape((members, 2, tokens), f32)],
        [loc, qh, gh, prefix],
        (),
        unit // 4,
    )
    gathered = lax.all_to_all(part, HEADS, 0, 0, tiled=True)
    gathered, kv3 = tied(gathered, kv3)
    da, block_grad, inverse = call(
        backward_kernel,
        [shape(head_major, bf16), shape(square, bf16), shape((tokens, width), f32)],
        [gathered, att, gh, qh],
        (),
        unit // 4,
    )
    back_pieces = spread(block_grad)
    have = jnp.minimum(position, WINDOW_BLOCKS - 1).astype(jnp.int32).reshape(1)
    normed, attended = call(
        softmax_kernel,
        [shape(query.shape, bf16), shape(query.shape, bf16)],
        [have, att, inverse, gain, query2, kv0, kv1, kv2, kv3],
        [flat_buffer],
        8 * unit,
        smem_first=True,
    )
    back_pieces, attended = tied(back_pieces, attended)
    back_totals = row_totals(back_pieces)
    (gq,) = call(
        query_gradient_kernel,
        [shape(query.shape, bf16)],
        [kh, vh, da, prefix],
        [flat_buffer],
        2 * unit,
    )
    back_totals, gq = tied(back_totals, gq)
    suffixes, da = tied(scanned(back_pieces, back_totals, True), da)
    suffix = spread(suffixes)
    pk, pv = call(
        key_value_local_kernel,
        [shape(head_major, f32)] * 2,
        [qh, kh, vh, da],
        (),
        4 * unit,
    )
    gk, gv = call(
        finish_kernel,
        [shape(query.shape, bf16)] * 2,
        [kh, vh, pk, pv, suffix],
        [flat_buffer, flat_buffer, token_buffer, token_buffer, copy_sems],
        unit // 2,
        hbm_out=(0, 1),
    )
    return normed, gq, gk, gv, attended


def solution(mesh):
    sizes = (4, 8, 4, 2)
    fine = Mesh(mesh.devices.reshape(sizes), ("y", "z", "x", "core"))
    tokens = P(CTX, HEADS, None)
    return jax.shard_map(
        local,
        mesh=fine,
        in_specs=(tokens, tokens, tokens, P(HEADS, None), tokens, tokens, tokens, tokens),
        out_specs=(tokens,) * 5,
        check_vma=False,
    )
```

```python
import functools
import jax
import jax.numpy as jnp
from jax import lax
from jax.experimental import pallas as pl
from jax.experimental.pallas import tpu as pltpu
from jax.sharding import Mesh, PartitionSpec as P

ATTN_HEADS = 64
HEAD_WIDTH = 128
WINDOW_BLOCKS = 4
CHANNELS = ATTN_HEADS * HEAD_WIDTH
EPSILON = 1e-06
LOG2E = 1.4426950408889634

f32 = jnp.float32
bf16 = jnp.bfloat16
MIB = 1 << 20
HEADS = ("x", "core")
CTX = ("y", "z")


def nn(a, b, precision=None):
    return lax.dot_general(
        a, b, (((1,), (0,)), ((), ())), precision=precision, preferred_element_type=f32
    )


def nt(a, b, precision=None):
    return lax.dot_general(
        a, b, (((1,), (1,)), ((), ())), precision=precision, preferred_element_type=f32
    )


def tn(a, b, precision=None):
    return lax.dot_general(
        a, b, (((0,), (0,)), ((), ())), precision=precision, preferred_element_type=f32
    )


def call(kernel, out_shapes, args, scratch=(), flops=0, smem_first=False, vmem=20, hbm_in=(), hbm_out=()):
    def place(i, far):
        return pl.BlockSpec(memory_space=pltpu.HBM if i in far else pltpu.VMEM)

    specs = [place(i, hbm_in) for i in range(len(args))]
    if smem_first:
        specs[0] = pl.BlockSpec(memory_space=pltpu.SMEM)
    moved = sum(a.size * a.dtype.itemsize for a in (*args, *out_shapes))
    return pl.pallas_call(
        kernel,
        out_shape=out_shapes,
        in_specs=specs,
        out_specs=[place(i, hbm_out) for i in range(len(out_shapes))],
        scratch_shapes=list(scratch),
        compiler_params=pltpu.CompilerParams(vmem_limit_bytes=vmem * MIB),
        cost_estimate=pl.CostEstimate(flops=flops, bytes_accessed=moved, transcendentals=0),
    )(*args)


def shape(dims, dtype):
    return jax.ShapeDtypeStruct(dims, dtype)


def fetch(pairs, sems):
    copies = []
    for i, (src, dst) in enumerate(pairs):
        copy = pltpu.make_async_copy(src, dst, sems.at[i])
        copy.start()
        copies.append(copy)
    return copies


def state_kernel(k_ref, v_ref, kh_ref, vh_ref, st_ref, ks, vs):
    tokens, heads, width = k_ref.shape
    ks[...] = k_ref[...].astype(f32).reshape(tokens * heads, width)
    vs[...] = v_ref[...].astype(f32).reshape(tokens * heads, width)
    for h in range(heads):
        kh = ks[pl.ds(h, tokens, stride=heads), :].astype(bf16)
        vh = vs[pl.ds(h, tokens, stride=heads), :].astype(bf16)
        kh_ref[h] = kh
        vh_ref[h] = vh
        st_ref[h] = tn(kh, vh).astype(bf16)


def each(count, body, unroll=8):
    def step(i, carry):
        body(i)
        return carry

    lax.fori_loop(0, count, step, 0, unroll=unroll)


def causal_below(rows):
    r = lax.broadcasted_iota(jnp.int32, (rows, rows), 0)
    c = lax.broadcasted_iota(jnp.int32, (rows, rows), 1)
    return c <= r


def local_kernel(q_ref, c_ref, gain_ref, kh_ref, vh_ref, qh_ref, gh_ref, loc_ref, qs, cs):
    tokens, heads, width = q_ref.shape
    half = tokens // 2
    qs[...] = q_ref[...].astype(f32).reshape(tokens * heads, width)
    cs[...] = (c_ref[...].astype(f32) * gain_ref[...][None]).reshape(tokens * heads, width)
    causal = causal_below(half)

    def head(h):
        qh = qs[pl.ds(h, tokens, stride=heads), :].astype(bf16)
        qh_ref[h] = qh
        gh_ref[h] = cs[pl.ds(h, tokens, stride=heads), :]
        kh = kh_ref[h]
        vh = vh_ref[h]
        w0 = jnp.where(causal, nt(qh[:half], kh[:half]), 0.0).astype(bf16)
        w10 = nt(qh[half:], kh[:half]).astype(bf16)
        w11 = jnp.where(causal, nt(qh[half:], kh[half:]), 0.0).astype(bf16)
        loc_ref[h, :half] = nn(w0, vh[:half])
        loc_ref[h, half:] = nn(w10, vh[:half]) + nn(w11, vh[half:])

    each(heads, head)


def attention_kernel(loc_ref, qh_ref, gh_ref, pre_ref, att_ref, part_ref):
    heads, tokens, width = loc_ref.shape
    squares = jnp.zeros((tokens, width), f32)
    inner = jnp.zeros((tokens, width), f32)
    for h in range(heads):
        att = loc_ref[h] + nn(qh_ref[h], pre_ref[h])
        att_ref[h] = att
        squares = squares + att * att
        inner = inner + att * gh_ref[h]
    ones = jnp.ones((8, width), f32)
    rows = jnp.concatenate(
        [
            nt(ones, squares, lax.Precision.HIGHEST)[0:1],
            nt(ones, inner, lax.Precision.HIGHEST)[0:1],
        ]
    )
    for j in range(part_ref.shape[0]):
        part_ref[j] = rows


def row_scales(g_ref):
    ones = jnp.ones((g_ref.shape[0], HEAD_WIDTH), f32)
    squares = tn(g_ref[:, 0, :], ones, lax.Precision.HIGHEST)
    inner = tn(g_ref[:, 1, :], ones, lax.Precision.HIGHEST)
    inverse = 1.0 / jnp.sqrt(squares / CHANNELS + EPSILON)
    return inverse, inverse * inner / CHANNELS


def backward_kernel(g_ref, att_ref, gh_ref, qh_ref, da_ref, bg_ref, inv_ref):
    inverse, mean = row_scales(g_ref)
    inv_ref[...] = inverse
    scaled = inverse * mean
    for h in range(att_ref.shape[0]):
        d = ((gh_ref[h] - att_ref[h] * scaled) * inverse).astype(bf16)
        da_ref[h] = d
        bg_ref[h] = tn(qh_ref[h], d).astype(bf16)


def softmax_kernel(
    pos_ref, att_ref, inv_ref, gain_ref, q2_ref, kv0, kv1, kv2, kv3,
    norm_hbm, out_hbm, norm, out, scratch, ahead, sems,
):
    heads, tokens, width = att_ref.shape
    kv = (kv0, kv1, kv2, kv3)
    inverse = inv_ref[...]
    for h in range(heads):
        scratch[pl.ds(h, tokens, stride=heads), :] = (
            gain_ref[h : h + 1, :] * (att_ref[h] * inverse)
        )
    norm[...] = scratch[...].astype(bf16).reshape(tokens, heads, width)
    writes = fetch([(norm, norm_hbm)], sems.at[pl.ds(4, 1)])

    scale = LOG2E * HEAD_WIDTH ** (-0.5)
    ones = jnp.ones((tokens, width), bf16)
    quarters = 4
    quarter = tokens // quarters

    def query_rows(chunk, rows):
        chunk_tokens = rows // heads
        t0 = pl.multiple_of(chunk * chunk_tokens, chunk_tokens)
        n = scratch[pl.ds(pl.multiple_of(chunk * rows, rows), rows), :].astype(bf16).astype(f32)
        q2 = q2_ref[pl.ds(t0, chunk_tokens)].astype(f32).reshape(rows, width)
        return (q2 + n).astype(bf16)

    def scores(chunk, rows, count):
        q = query_rows(chunk, rows)
        row = chunk * rows + lax.broadcasted_iota(jnp.int32, (rows, tokens), 0)
        column = lax.broadcasted_iota(jnp.int32, (rows, tokens), 1)
        own = jnp.where(column <= row // heads, nt(q, kv[0][0]), -1e30)
        return [own] + [nt(q, kv[b][0]) for b in range(1, count)]

    def weigh(parts, chunk, rows):
        top = None
        for s in parts:
            for j in range(0, tokens, 128):
                piece = s[:, j : j + 128]
                top = piece if top is None else jnp.maximum(top, piece)
        top = jnp.max(top, axis=1, keepdims=True) * scale
        total = None
        for b, s in enumerate(parts):
            p = jnp.exp2(s * scale - top).astype(bf16)
            o = nn(p, jnp.concatenate([kv[b][1], ones], axis=1))
            total = o if total is None else total + o
        chunk_tokens = rows // heads
        t0 = pl.multiple_of(chunk * chunk_tokens, chunk_tokens)
        out[pl.ds(t0, chunk_tokens)] = (
            (total[:, :width] / total[:, width:]).astype(bf16).reshape(chunk_tokens, heads, width)
        )

    def store(i):
        part = pl.ds(pl.multiple_of(i * quarter, quarter), quarter)
        return pltpu.make_async_copy(out.at[part], out_hbm.at[part], sems.at[i])

    def run(count):
        rows = 256
        per = quarter * heads // rows

        def body(i, carry):
            for j in range(per):
                chunk = i * per + j
                weigh(scores(chunk, rows, count), chunk, rows)
            store(i).start()
            return carry

        lax.fori_loop(0, quarters, body, 0)

    def run_ahead():
        rows = 512
        per = quarter * heads // rows
        last = quarters * per - 1

        def put(slot, chunk):
            for b, s in enumerate(scores(chunk, rows, WINDOW_BLOCKS)):
                ahead[slot, b] = s

        def body(i, carry):
            for j in range(per):
                chunk = i * per + j
                put((j + 1) % 2, jnp.minimum(chunk + 1, last))
                weigh([ahead[j % 2, b] for b in range(WINDOW_BLOCKS)], chunk, rows)
            store(i).start()
            return carry

        put(0, 0)
        lax.fori_loop(0, quarters, body, 0)

    have = pos_ref[0]
    for count in range(1, WINDOW_BLOCKS):
        pl.when(have == count - 1)(functools.partial(run, count))
    pl.when(have == WINDOW_BLOCKS - 1)(run_ahead)
    for i in range(quarters):
        store(i).wait()
    writes[0].wait()


def query_gradient_kernel(kh_ref, vh_ref, da_ref, pre_ref, gq_hbm, qs, out, sems):
    heads, tokens, width = kh_ref.shape
    half = tokens // 2
    below = causal_below(half)
    lo, hi = slice(0, half), slice(half, tokens)

    def head(h):
        k, v, da = kh_ref[h], vh_ref[h], da_ref[h]
        d00 = jnp.where(below, nt(da[lo], v[lo]), 0.0).astype(bf16)
        d10 = nt(da[hi], v[lo]).astype(bf16)
        d11 = jnp.where(below, nt(da[hi], v[hi]), 0.0).astype(bf16)
        gq = nt(da, pre_ref[h])
        qs[pl.ds(h, half, stride=heads), :] = gq[lo] + nn(d00, k[lo])
        qs[pl.ds(half * heads + h, half, stride=heads), :] = (
            gq[hi] + nn(d10, k[lo]) + nn(d11, k[hi])
        )

    each(heads, head)
    pieces = sems.shape[0]
    rows = tokens // pieces
    copies = []
    for i in range(pieces):
        part = pl.ds(i * rows, rows)
        out[part] = (
            qs[pl.ds(i * rows * heads, rows * heads), :].astype(bf16).reshape(rows, heads, width)
        )
        copies += fetch([(out.at[part], gq_hbm.at[part])], sems.at[pl.ds(i, 1)])
    for copy in copies:
        copy.wait()


def key_value_local_kernel(qh_ref, kh_ref, vh_ref, da_ref, gk_ref, gv_ref):
    heads, tokens, width = qh_ref.shape
    half = tokens // 2
    r = lax.broadcasted_iota(jnp.int32, (half, half), 0)
    c = lax.broadcasted_iota(jnp.int32, (half, half), 1)
    above = r <= c
    lo, hi = slice(0, half), slice(half, tokens)

    def up(x):
        return jnp.where(above, x, 0.0).astype(bf16)

    def head(h):
        q, k, v, da = qh_ref[h], kh_ref[h], vh_ref[h], da_ref[h]
        for out, a, b, other in ((gk_ref, v, da, q), (gv_ref, k, q, da)):
            m00 = up(nt(a[lo], b[lo]))
            m01 = nt(a[lo], b[hi]).astype(bf16)
            m11 = up(nt(a[hi], b[hi]))
            out[h, :half] = nn(m00, other[lo]) + nn(m01, other[hi])
            out[h, half:] = nn(m11, other[hi])

    each(heads, head)


def finish_kernel(
    kh_ref, vh_ref, pk_ref, pv_ref, suf_ref, gk_hbm, gv_hbm, ks, vs, kb, vb, sems
):
    heads, tokens, width = kh_ref.shape
    pieces = sems.shape[0] // 2
    rows = tokens // pieces
    copies = []
    for i in range(pieces):
        part = pl.ds(i * rows, rows)
        for h in range(heads):
            suf = suf_ref[h]
            target = pl.ds(i * rows * heads + h, rows, stride=heads)
            ks[target, :] = pk_ref[h, part] + nt(vh_ref[h, part], suf)
            vs[target, :] = pv_ref[h, part] + nn(kh_ref[h, part], suf)
        flat = pl.ds(i * rows * heads, rows * heads)
        for src, buffer in ((ks, kb), (vs, vb)):
            buffer[part] = src[flat, :].astype(bf16).reshape(rows, heads, width)
        copies += fetch(
            [(kb.at[part], gk_hbm.at[part]), (vb.at[part], gv_hbm.at[part])],
            sems.at[pl.ds(2 * i, 2)],
        )
    for copy in copies:
        copy.wait()


def scan_kernel(back, recv_ref, t1_ref, t2_ref, t3_ref, out_ref):
    count = recv_ref.shape[0]
    running = t1_ref[...].astype(f32) + t2_ref[...].astype(f32) + t3_ref[...].astype(f32)
    order = range(count - 1, -1, -1) if back else range(count)
    for i in order:
        out_ref[i] = running.astype(bf16)
        running = running + recv_ref[i].astype(f32)


def total_kernel(recv_ref, *refs):
    *sources, out_ref = refs[:3]
    for j, source in enumerate(sources):
        refs[3][j] = source[...]
    total = recv_ref[0].astype(f32)
    for i in range(1, recv_ref.shape[0]):
        total = total + recv_ref[i].astype(f32)
    out_ref[...] = total.astype(bf16)


def tied(*values):
    return lax.optimization_barrier(values)


def row_total(pieces):
    return call(total_kernel, [shape(pieces.shape[1:], bf16)], [pieces])[0]


def other_rows(total, back):
    rows = lax.axis_size("y")
    got = []
    for d in (2, 1, 3):
        pairs = [(i + d, i) if back else (i, i + d) for i in range(rows - d)]
        got.append(lax.ppermute(total, "y", pairs))
    return got


def scanned(pieces, totals, back):
    return call(
        functools.partial(scan_kernel, back), [shape(pieces.shape, bf16)], [pieces, *totals]
    )[0]


def spread(x):
    return lax.all_to_all(x, "z", 0, 0, tiled=True)


def local(query, key, value, gain, cotangent, query2, key2, softmax_values):
    tokens, heads, width = query.shape
    flat = (tokens * heads, width)
    head_major = (heads, tokens, width)
    square = (heads, width, width)
    unit = 2 * tokens * tokens * width * heads
    ring = lax.axis_size(CTX)
    members = lax.axis_size(HEADS)
    token_buffer = pltpu.VMEM(query.shape, bf16)
    flat_buffer = pltpu.VMEM(flat, f32)

    def sems(n):
        return pltpu.SemaphoreType.DMA((n,))

    def onward(x):
        return lax.ppermute(x, CTX, [(i, i + 1) for i in range(ring - 1)])

    have = jnp.minimum(lax.axis_index(CTX), WINDOW_BLOCKS - 1).astype(jnp.int32).reshape(1)
    key, value, have = tied(key, value, have)

    kh, vh, states = call(
        state_kernel,
        [shape(head_major, bf16), shape(head_major, bf16), shape(square, bf16)],
        [key, value],
        [flat_buffer, flat_buffer],
        unit // 4,
    )
    states, query, cotangent = tied(states, query, cotangent)
    pieces, kh, vh = tied(spread(states), kh, vh)
    total, kv0 = call(
        total_kernel,
        [shape(square[1:], bf16), shape((2, tokens, width), bf16)],
        [pieces, key2[:, 0], softmax_values[:, 0]],
    )
    total, kh, vh = tied(total, kh, vh)
    totals = other_rows(total, False)
    kv1 = onward(kv0)
    qh, gh, loc = call(
        local_kernel,
        [shape(head_major, bf16), shape(head_major, f32), shape(head_major, f32)],
        [query, cotangent, gain, kh, vh],
        [flat_buffer, flat_buffer],
        2 * unit,
    )
    *totals, kv1, loc = tied(*totals, kv1, loc)
    prefix, kv1 = tied(spread(scanned(pieces, totals, False)), kv1)
    kv2 = onward(kv1)
    att, part = call(
        attention_kernel,
        [shape(head_major, f32), shape((members, 2, tokens), f32)],
        [loc, qh, gh, prefix],
        (),
        unit // 4,
    )
    gathered = lax.all_to_all(part, HEADS, 0, 0, tiled=True)
    gathered, kv2 = tied(gathered, kv2)
    da, block_grad, inverse = call(
        backward_kernel,
        [shape(head_major, bf16), shape(square, bf16), shape((tokens, width), f32)],
        [gathered, att, gh, qh],
        (),
        unit // 4,
    )
    back_pieces, att, da, inverse, kv2 = tied(spread(block_grad), att, da, inverse, kv2)
    back_total, att, da, inverse, kv2 = tied(row_total(back_pieces), att, da, inverse, kv2)
    kv3 = onward(kv2)
    back_totals = other_rows(back_total, True)
    normed, attended = call(
        softmax_kernel,
        [shape(query.shape, bf16), shape(query.shape, bf16)],
        [have, att, inverse, gain, query2, kv0, kv1, kv2, kv3],
        [
            token_buffer,
            token_buffer,
            flat_buffer,
            pltpu.VMEM((2, WINDOW_BLOCKS, tokens, tokens), f32),
            sems(5),
        ],
        8 * unit,
        smem_first=True,
        vmem=40,
        hbm_out=(0, 1),
    )
    (gq,) = call(
        query_gradient_kernel,
        [shape(query.shape, bf16)],
        [kh, vh, da, prefix],
        [flat_buffer, token_buffer, sems(4)],
        2 * unit,
        hbm_out=(0,),
    )
    pk, pv = call(
        key_value_local_kernel, [shape(head_major, f32)] * 2, [qh, kh, vh, da], (), 4 * unit
    )
    *back_totals, normed, attended, gq, pk, pv = tied(
        *back_totals, normed, attended, gq, pk, pv
    )
    suffix = spread(scanned(back_pieces, back_totals, True))
    gk, gv = call(
        finish_kernel,
        [shape(query.shape, bf16)] * 2,
        [kh, vh, pk, pv, suffix],
        [flat_buffer, flat_buffer, token_buffer, token_buffer, sems(8)],
        unit // 2,
        hbm_out=(0, 1),
    )
    return normed, gq, gk, gv, attended


def solution(mesh):
    sizes = (4, 8, 4, 2)
    fine = Mesh(mesh.devices.reshape(sizes), ("y", "z", "x", "core"))
    tokens = P(CTX, HEADS, None)
    return jax.shard_map(
        local,
        mesh=fine,
        in_specs=(tokens, tokens, tokens, P(HEADS, None), tokens, tokens, tokens, tokens),
        out_specs=(tokens,) * 5,
        check_vma=False,
    )
```

```python
import functools
import jax
import jax.numpy as jnp
from jax import lax
from jax.experimental import pallas as pl
from jax.experimental.pallas import tpu as pltpu
from jax.sharding import Mesh, PartitionSpec as P

ATTN_HEADS = 64
HEAD_WIDTH = 128
WINDOW_BLOCKS = 4
CHANNELS = ATTN_HEADS * HEAD_WIDTH
EPSILON = 1e-06
LOG2E = 1.4426950408889634

f32 = jnp.float32
bf16 = jnp.bfloat16
MIB = 1 << 20
HEADS = ("x", "core")
CTX = ("y", "z")


def nn(a, b, precision=None):
    return lax.dot_general(
        a, b, (((1,), (0,)), ((), ())), precision=precision, preferred_element_type=f32
    )


def nt(a, b, precision=None):
    return lax.dot_general(
        a, b, (((1,), (1,)), ((), ())), precision=precision, preferred_element_type=f32
    )


def tn(a, b, precision=None):
    return lax.dot_general(
        a, b, (((0,), (0,)), ((), ())), precision=precision, preferred_element_type=f32
    )


def call(kernel, out_shapes, args, scratch=(), flops=0, smem_first=False, vmem=20, hbm_in=(), hbm_out=()):
    def place(i, far):
        return pl.BlockSpec(memory_space=pltpu.HBM if i in far else pltpu.VMEM)

    specs = [place(i, hbm_in) for i in range(len(args))]
    if smem_first:
        specs[0] = pl.BlockSpec(memory_space=pltpu.SMEM)
    moved = sum(a.size * a.dtype.itemsize for a in (*args, *out_shapes))
    return pl.pallas_call(
        kernel,
        out_shape=out_shapes,
        in_specs=specs,
        out_specs=[place(i, hbm_out) for i in range(len(out_shapes))],
        scratch_shapes=list(scratch),
        compiler_params=pltpu.CompilerParams(vmem_limit_bytes=vmem * MIB),
        cost_estimate=pl.CostEstimate(flops=flops, bytes_accessed=moved, transcendentals=0),
    )(*args)


def shape(dims, dtype):
    return jax.ShapeDtypeStruct(dims, dtype)


def fetch(pairs, sems):
    copies = []
    for i, (src, dst) in enumerate(pairs):
        copy = pltpu.make_async_copy(src, dst, sems.at[i])
        copy.start()
        copies.append(copy)
    return copies


def state_kernel(k_ref, v_ref, kh_ref, vh_ref, st_ref, ks, vs):
    tokens, heads, width = k_ref.shape
    ks[...] = k_ref[...].astype(f32).reshape(tokens * heads, width)
    vs[...] = v_ref[...].astype(f32).reshape(tokens * heads, width)
    for h in range(heads):
        kh = ks[pl.ds(h, tokens, stride=heads), :].astype(bf16)
        vh = vs[pl.ds(h, tokens, stride=heads), :].astype(bf16)
        kh_ref[h] = kh
        vh_ref[h] = vh
        st_ref[h] = tn(kh, vh).astype(bf16)


def each(count, body, unroll=8):
    def step(i, carry):
        body(i)
        return carry

    lax.fori_loop(0, count, step, 0, unroll=unroll)


def causal_below(rows):
    r = lax.broadcasted_iota(jnp.int32, (rows, rows), 0)
    c = lax.broadcasted_iota(jnp.int32, (rows, rows), 1)
    return c <= r


def local_kernel(q_ref, c_ref, gain_ref, kh_ref, vh_ref, qh_ref, gh_ref, loc_ref, qs, cs):
    tokens, heads, width = q_ref.shape
    half = tokens // 2
    qs[...] = q_ref[...].astype(f32).reshape(tokens * heads, width)
    cs[...] = (c_ref[...].astype(f32) * gain_ref[...][None]).reshape(tokens * heads, width)
    causal = causal_below(half)

    def head(h):
        qh = qs[pl.ds(h, tokens, stride=heads), :].astype(bf16)
        qh_ref[h] = qh
        gh_ref[h] = cs[pl.ds(h, tokens, stride=heads), :]
        kh = kh_ref[h]
        vh = vh_ref[h]
        w0 = jnp.where(causal, nt(qh[:half], kh[:half]), 0.0).astype(bf16)
        w10 = nt(qh[half:], kh[:half]).astype(bf16)
        w11 = jnp.where(causal, nt(qh[half:], kh[half:]), 0.0).astype(bf16)
        loc_ref[h, :half] = nn(w0, vh[:half])
        loc_ref[h, half:] = nn(w10, vh[:half]) + nn(w11, vh[half:])

    each(heads, head)


def attention_kernel(loc_ref, qh_ref, gh_ref, pre_ref, att_ref, part_ref):
    heads, tokens, width = loc_ref.shape
    squares = jnp.zeros((tokens, width), f32)
    inner = jnp.zeros((tokens, width), f32)
    for h in range(heads):
        att = loc_ref[h] + nn(qh_ref[h], pre_ref[h])
        att_ref[h] = att
        squares = squares + att * att
        inner = inner + att * gh_ref[h]
    ones = jnp.ones((8, width), f32)
    rows = jnp.concatenate(
        [
            nt(ones, squares, lax.Precision.HIGHEST)[0:1],
            nt(ones, inner, lax.Precision.HIGHEST)[0:1],
        ]
    )
    for j in range(part_ref.shape[0]):
        part_ref[j] = rows


def row_scales(g_ref):
    ones = jnp.ones((g_ref.shape[0], HEAD_WIDTH), f32)
    squares = tn(g_ref[:, 0, :], ones, lax.Precision.HIGHEST)
    inner = tn(g_ref[:, 1, :], ones, lax.Precision.HIGHEST)
    inverse = 1.0 / jnp.sqrt(squares / CHANNELS + EPSILON)
    return inverse, inverse * inner / CHANNELS


def backward_kernel(g_ref, att_ref, gh_ref, qh_ref, da_ref, bg_ref, inv_ref):
    inverse, mean = row_scales(g_ref)
    inv_ref[...] = inverse
    scaled = inverse * mean
    for h in range(att_ref.shape[0]):
        d = ((gh_ref[h] - att_ref[h] * scaled) * inverse).astype(bf16)
        da_ref[h] = d
        bg_ref[h] = tn(qh_ref[h], d).astype(bf16)


def softmax_kernel(
    pos_ref, att_ref, inv_ref, gain_ref, q2_ref, kv0, kv1, kv2, kv3,
    norm_hbm, out_hbm, norm, out, scratch, ahead, sems,
):
    heads, tokens, width = att_ref.shape
    kv = (kv0, kv1, kv2, kv3)
    inverse = inv_ref[...]
    for h in range(heads):
        scratch[pl.ds(h, tokens, stride=heads), :] = (
            gain_ref[h : h + 1, :] * (att_ref[h] * inverse)
        )
    norm[...] = scratch[...].astype(bf16).reshape(tokens, heads, width)
    writes = fetch([(norm, norm_hbm)], sems.at[pl.ds(4, 1)])

    scale = LOG2E * HEAD_WIDTH ** (-0.5)
    ones = jnp.ones((tokens, width), bf16)
    quarters = 4
    quarter = tokens // quarters

    def query_rows(chunk, rows):
        chunk_tokens = rows // heads
        t0 = pl.multiple_of(chunk * chunk_tokens, chunk_tokens)
        n = scratch[pl.ds(pl.multiple_of(chunk * rows, rows), rows), :].astype(bf16).astype(f32)
        q2 = q2_ref[pl.ds(t0, chunk_tokens)].astype(f32).reshape(rows, width)
        return (q2 + n).astype(bf16)

    def scores(chunk, rows, count):
        q = query_rows(chunk, rows)
        row = chunk * rows + lax.broadcasted_iota(jnp.int32, (rows, tokens), 0)
        column = lax.broadcasted_iota(jnp.int32, (rows, tokens), 1)
        own = jnp.where(column <= row // heads, nt(q, kv[0][0]), -1e30)
        return [own] + [nt(q, kv[b][0]) for b in range(1, count)]

    def weigh(parts, chunk, rows):
        top = None
        for s in parts:
            for j in range(0, tokens, 128):
                piece = s[:, j : j + 128]
                top = piece if top is None else jnp.maximum(top, piece)
        top = jnp.max(top, axis=1, keepdims=True) * scale
        total = None
        for b, s in enumerate(parts):
            p = jnp.exp2(s * scale - top).astype(bf16)
            o = nn(p, jnp.concatenate([kv[b][1], ones], axis=1))
            total = o if total is None else total + o
        chunk_tokens = rows // heads
        t0 = pl.multiple_of(chunk * chunk_tokens, chunk_tokens)
        out[pl.ds(t0, chunk_tokens)] = (
            (total[:, :width] / total[:, width:]).astype(bf16).reshape(chunk_tokens, heads, width)
        )

    def store(i):
        part = pl.ds(pl.multiple_of(i * quarter, quarter), quarter)
        return pltpu.make_async_copy(out.at[part], out_hbm.at[part], sems.at[i])

    def run(count):
        rows = 256
        per = quarter * heads // rows

        def body(i, carry):
            for j in range(per):
                chunk = i * per + j
                weigh(scores(chunk, rows, count), chunk, rows)
            store(i).start()
            return carry

        lax.fori_loop(0, quarters, body, 0)

    def run_ahead():
        rows = 512
        per = quarter * heads // rows
        last = quarters * per - 1

        def put(slot, chunk):
            for b, s in enumerate(scores(chunk, rows, WINDOW_BLOCKS)):
                ahead[slot, b] = s

        def body(i, carry):
            for j in range(per):
                chunk = i * per + j
                put((j + 1) % 2, jnp.minimum(chunk + 1, last))
                weigh([ahead[j % 2, b] for b in range(WINDOW_BLOCKS)], chunk, rows)
            store(i).start()
            return carry

        put(0, 0)
        lax.fori_loop(0, quarters, body, 0)

    have = pos_ref[0]
    for count in range(1, WINDOW_BLOCKS):
        pl.when(have == count - 1)(functools.partial(run, count))
    pl.when(have == WINDOW_BLOCKS - 1)(run_ahead)
    for i in range(quarters):
        store(i).wait()
    writes[0].wait()


def query_gradient_kernel(kh_ref, vh_ref, da_ref, pre_ref, gq_hbm, qs, out, sems):
    heads, tokens, width = kh_ref.shape
    half = tokens // 2
    below = causal_below(half)
    lo, hi = slice(0, half), slice(half, tokens)

    def head(h):
        k, v, da = kh_ref[h], vh_ref[h], da_ref[h]
        d00 = jnp.where(below, nt(da[lo], v[lo]), 0.0).astype(bf16)
        d10 = nt(da[hi], v[lo]).astype(bf16)
        d11 = jnp.where(below, nt(da[hi], v[hi]), 0.0).astype(bf16)
        gq = nt(da, pre_ref[h])
        qs[pl.ds(h, half, stride=heads), :] = gq[lo] + nn(d00, k[lo])
        qs[pl.ds(half * heads + h, half, stride=heads), :] = (
            gq[hi] + nn(d10, k[lo]) + nn(d11, k[hi])
        )

    each(heads, head)
    pieces = sems.shape[0]
    rows = tokens // pieces
    copies = []
    for i in range(pieces):
        part = pl.ds(i * rows, rows)
        out[part] = (
            qs[pl.ds(i * rows * heads, rows * heads), :].astype(bf16).reshape(rows, heads, width)
        )
        copies += fetch([(out.at[part], gq_hbm.at[part])], sems.at[pl.ds(i, 1)])
    for copy in copies:
        copy.wait()


def key_value_local_kernel(qh_ref, kh_ref, vh_ref, da_ref, gk_ref, gv_ref):
    heads, tokens, width = qh_ref.shape
    half = tokens // 2
    r = lax.broadcasted_iota(jnp.int32, (half, half), 0)
    c = lax.broadcasted_iota(jnp.int32, (half, half), 1)
    above = r <= c
    lo, hi = slice(0, half), slice(half, tokens)

    def up(x):
        return jnp.where(above, x, 0.0).astype(bf16)

    def head(h):
        q, k, v, da = qh_ref[h], kh_ref[h], vh_ref[h], da_ref[h]
        for out, a, b, other in ((gk_ref, v, da, q), (gv_ref, k, q, da)):
            m00 = up(nt(a[lo], b[lo]))
            m01 = nt(a[lo], b[hi]).astype(bf16)
            m11 = up(nt(a[hi], b[hi]))
            out[h, :half] = nn(m00, other[lo]) + nn(m01, other[hi])
            out[h, half:] = nn(m11, other[hi])

    each(heads, head)


def finish_kernel(
    kh_ref, vh_ref, pk_ref, pv_ref, suf_ref, gk_hbm, gv_hbm, ks, vs, kb, vb, sems
):
    heads, tokens, width = kh_ref.shape
    pieces = sems.shape[0] // 2
    rows = tokens // pieces
    copies = []
    for i in range(pieces):
        part = pl.ds(i * rows, rows)
        for h in range(heads):
            suf = suf_ref[h]
            target = pl.ds(i * rows * heads + h, rows, stride=heads)
            ks[target, :] = pk_ref[h, part] + nt(vh_ref[h, part], suf)
            vs[target, :] = pv_ref[h, part] + nn(kh_ref[h, part], suf)
        flat = pl.ds(i * rows * heads, rows * heads)
        for src, buffer in ((ks, kb), (vs, vb)):
            buffer[part] = src[flat, :].astype(bf16).reshape(rows, heads, width)
        copies += fetch(
            [(kb.at[part], gk_hbm.at[part]), (vb.at[part], gv_hbm.at[part])],
            sems.at[pl.ds(2 * i, 2)],
        )
    for copy in copies:
        copy.wait()


def scan_kernel(back, recv_ref, *refs):
    *others, out_ref = refs
    count = recv_ref.shape[0]
    running = sum(other[...].astype(f32) for other in others)
    order = range(count) if back else range(count - 1, -1, -1)
    for i in order:
        out_ref[i] = running.astype(bf16)
        running = running + recv_ref[i].astype(f32)


def pair_kernel(own_ref, other_ref, out_ref):
    out_ref[...] = (own_ref[...].astype(f32) + other_ref[...].astype(f32)).astype(bf16)


def total_kernel(recv_ref, *refs):
    *sources, out_ref = refs[:3]
    for j, source in enumerate(sources):
        refs[3][j] = source[...]
    total = recv_ref[0].astype(f32)
    for i in range(1, recv_ref.shape[0]):
        total = total + recv_ref[i].astype(f32)
    out_ref[...] = total.astype(bf16)


def tied(*values):
    return lax.optimization_barrier(values)


def row_total(pieces):
    return call(total_kernel, [shape(pieces.shape[1:], bf16)], [pieces])[0]


def from_row(x, d, back):
    rows = lax.axis_size("y")
    return lax.ppermute(x, "y", [(i + d, i) if back else (i, i + d) for i in range(rows - d)])


def pair_total(own, other):
    return call(pair_kernel, [shape(own.shape, bf16)], [own, other])[0]


def scanned(pieces, totals, back):
    return call(
        functools.partial(scan_kernel, back), [shape(pieces.shape, bf16)], [pieces, *totals]
    )[0]


def spread(x):
    members = list(range(lax.axis_size("z")))[::-1]
    return lax.all_to_all(x, "z", 0, 0, tiled=True, axis_index_groups=[members])


def local(query, key, value, gain, cotangent, query2, key2, softmax_values):
    tokens, heads, width = query.shape
    flat = (tokens * heads, width)
    head_major = (heads, tokens, width)
    square = (heads, width, width)
    unit = 2 * tokens * tokens * width * heads
    ring = lax.axis_size(CTX)
    members = lax.axis_size(HEADS)
    token_buffer = pltpu.VMEM(query.shape, bf16)
    flat_buffer = pltpu.VMEM(flat, f32)

    def sems(n):
        return pltpu.SemaphoreType.DMA((n,))

    def onward(x):
        return lax.ppermute(x, CTX, [(i, i + 1) for i in range(ring - 1)])

    have = jnp.minimum(lax.axis_index(CTX), WINDOW_BLOCKS - 1).astype(jnp.int32).reshape(1)
    key, value, have = tied(key, value, have)

    kh, vh, states = call(
        state_kernel,
        [shape(head_major, bf16), shape(head_major, bf16), shape(square, bf16)],
        [key, value],
        [flat_buffer, flat_buffer],
        unit // 4,
    )
    states, query, cotangent = tied(states, query, cotangent)
    pieces, kh, vh = tied(spread(states), kh, vh)
    total, kv0 = call(
        total_kernel,
        [shape(square[1:], bf16), shape((2, tokens, width), bf16)],
        [pieces, key2[:, 0], softmax_values[:, 0]],
    )
    total, kh, vh = tied(total, kh, vh)
    totals = [from_row(total, d, False) for d in (2, 1, 3)]
    kv1 = onward(kv0)
    qh, gh, loc = call(
        local_kernel,
        [shape(head_major, bf16), shape(head_major, f32), shape(head_major, f32)],
        [query, cotangent, gain, kh, vh],
        [flat_buffer, flat_buffer],
        2 * unit,
    )
    *totals, kv1, loc = tied(*totals, kv1, loc)
    prefix, kv1 = tied(spread(scanned(pieces, totals, False)), kv1)
    kv2 = onward(kv1)
    att, part = call(
        attention_kernel,
        [shape(head_major, f32), shape((members, 2, tokens), f32)],
        [loc, qh, gh, prefix],
        (),
        unit // 4,
    )
    gathered = lax.all_to_all(part, HEADS, 0, 0, tiled=True)
    gathered, kv2 = tied(gathered, kv2)
    da, block_grad, inverse = call(
        backward_kernel,
        [shape(head_major, bf16), shape(square, bf16), shape((tokens, width), f32)],
        [gathered, att, gh, qh],
        (),
        unit // 4,
    )
    back_pieces, att, da, inverse, kv2 = tied(spread(block_grad), att, da, inverse, kv2)
    kv3 = onward(kv2)
    (gq,) = call(
        query_gradient_kernel,
        [shape(query.shape, bf16)],
        [kh, vh, da, prefix],
        [flat_buffer, token_buffer, sems(4)],
        2 * unit,
        hbm_out=(0,),
    )
    back_total, gq, da = tied(row_total(back_pieces), gq, da)
    back_near = from_row(back_total, 1, True)
    pk, pv = call(
        key_value_local_kernel, [shape(head_major, f32)] * 2, [qh, kh, vh, da], (), 4 * unit
    )
    back_near, pk, pv, att = tied(back_near, pk, pv, att)
    back_far = from_row(pair_total(back_total, back_near), 2, True)
    normed, attended = call(
        softmax_kernel,
        [shape(query.shape, bf16), shape(query.shape, bf16)],
        [have, att, inverse, gain, query2, kv0, kv1, kv2, kv3],
        [
            token_buffer,
            token_buffer,
            flat_buffer,
            pltpu.VMEM((2, WINDOW_BLOCKS, tokens, tokens), f32),
            sems(5),
        ],
        8 * unit,
        smem_first=True,
        vmem=40,
        hbm_out=(0, 1),
    )
    back_far, normed, attended, gq = tied(back_far, normed, attended, gq)
    suffix = spread(scanned(back_pieces, [back_near, back_far], True))
    gk, gv = call(
        finish_kernel,
        [shape(query.shape, bf16)] * 2,
        [kh, vh, pk, pv, suffix],
        [flat_buffer, flat_buffer, token_buffer, token_buffer, sems(8)],
        unit // 2,
        hbm_out=(0, 1),
    )
    return normed, gq, gk, gv, attended


def solution(mesh):
    sizes = (4, 8, 4, 2)
    fine = Mesh(mesh.devices.reshape(sizes), ("y", "z", "x", "core"))
    tokens = P(CTX, HEADS, None)
    return jax.shard_map(
        local,
        mesh=fine,
        in_specs=(tokens, tokens, tokens, P(HEADS, None), tokens, tokens, tokens, tokens),
        out_specs=(tokens,) * 5,
        check_vma=False,
    )
```

```python
import functools
import jax
import jax.numpy as jnp
from jax import lax
from jax.experimental import pallas as pl
from jax.experimental.pallas import tpu as pltpu
from jax.sharding import Mesh, PartitionSpec as P

ATTN_HEADS = 64
HEAD_WIDTH = 128
WINDOW_BLOCKS = 4
CHANNELS = ATTN_HEADS * HEAD_WIDTH
EPSILON = 1e-06
LOG2E = 1.4426950408889634

f32 = jnp.float32
bf16 = jnp.bfloat16
MIB = 1 << 20
HEADS = ("x", "core")
CTX = ("y", "z")


def nn(a, b, precision=None):
    return lax.dot_general(
        a, b, (((1,), (0,)), ((), ())), precision=precision, preferred_element_type=f32
    )


def nt(a, b, precision=None):
    return lax.dot_general(
        a, b, (((1,), (1,)), ((), ())), precision=precision, preferred_element_type=f32
    )


def tn(a, b, precision=None):
    return lax.dot_general(
        a, b, (((0,), (0,)), ((), ())), precision=precision, preferred_element_type=f32
    )


def call(kernel, out_shapes, args, scratch=(), flops=0, smem_first=False, vmem=20, hbm_in=(), hbm_out=()):
    def place(i, far):
        return pl.BlockSpec(memory_space=pltpu.HBM if i in far else pltpu.VMEM)

    specs = [place(i, hbm_in) for i in range(len(args))]
    if smem_first:
        specs[0] = pl.BlockSpec(memory_space=pltpu.SMEM)
    moved = sum(a.size * a.dtype.itemsize for a in (*args, *out_shapes))
    return pl.pallas_call(
        kernel,
        out_shape=out_shapes,
        in_specs=specs,
        out_specs=[place(i, hbm_out) for i in range(len(out_shapes))],
        scratch_shapes=list(scratch),
        compiler_params=pltpu.CompilerParams(vmem_limit_bytes=vmem * MIB),
        cost_estimate=pl.CostEstimate(flops=flops, bytes_accessed=moved, transcendentals=0),
    )(*args)


def shape(dims, dtype):
    return jax.ShapeDtypeStruct(dims, dtype)


def fetch(pairs, sems):
    copies = []
    for i, (src, dst) in enumerate(pairs):
        copy = pltpu.make_async_copy(src, dst, sems.at[i])
        copy.start()
        copies.append(copy)
    return copies


def state_kernel(k_ref, v_ref, kh_ref, vh_ref, st_ref, ks, vs):
    tokens, heads, width = k_ref.shape
    ks[...] = k_ref[...].astype(f32).reshape(tokens * heads, width)
    vs[...] = v_ref[...].astype(f32).reshape(tokens * heads, width)
    for h in range(heads):
        kh = ks[pl.ds(h, tokens, stride=heads), :].astype(bf16)
        vh = vs[pl.ds(h, tokens, stride=heads), :].astype(bf16)
        kh_ref[h] = kh
        vh_ref[h] = vh
        st_ref[h] = tn(kh, vh).astype(bf16)


def each(count, body, unroll=8):
    def step(i, carry):
        body(i)
        return carry

    lax.fori_loop(0, count, step, 0, unroll=unroll)


def causal_below(rows):
    r = lax.broadcasted_iota(jnp.int32, (rows, rows), 0)
    c = lax.broadcasted_iota(jnp.int32, (rows, rows), 1)
    return c <= r


def local_kernel(q_ref, c_ref, gain_ref, kh_ref, vh_ref, qh_ref, gh_ref, loc_ref, qs, cs):
    tokens, heads, width = q_ref.shape
    half = tokens // 2
    qs[...] = q_ref[...].astype(f32).reshape(tokens * heads, width)
    cs[...] = (c_ref[...].astype(f32) * gain_ref[...][None]).reshape(tokens * heads, width)
    causal = causal_below(half)

    def head(h):
        qh = qs[pl.ds(h, tokens, stride=heads), :].astype(bf16)
        qh_ref[h] = qh
        gh_ref[h] = cs[pl.ds(h, tokens, stride=heads), :]
        kh = kh_ref[h]
        vh = vh_ref[h]
        w0 = jnp.where(causal, nt(qh[:half], kh[:half]), 0.0).astype(bf16)
        w10 = nt(qh[half:], kh[:half]).astype(bf16)
        w11 = jnp.where(causal, nt(qh[half:], kh[half:]), 0.0).astype(bf16)
        loc_ref[h, :half] = nn(w0, vh[:half])
        loc_ref[h, half:] = nn(w10, vh[:half]) + nn(w11, vh[half:])

    each(heads, head)


def attention_kernel(loc_ref, qh_ref, gh_ref, pre_ref, att_ref, part_ref):
    heads, tokens, width = loc_ref.shape
    squares = jnp.zeros((tokens, width), f32)
    inner = jnp.zeros((tokens, width), f32)
    for h in range(heads):
        att = loc_ref[h] + nn(qh_ref[h], pre_ref[h])
        att_ref[h] = att
        squares = squares + att * att
        inner = inner + att * gh_ref[h]
    ones = jnp.ones((8, width), f32)
    rows = jnp.concatenate(
        [
            nt(ones, squares, lax.Precision.HIGHEST)[0:1],
            nt(ones, inner, lax.Precision.HIGHEST)[0:1],
        ]
    )
    for j in range(part_ref.shape[0]):
        part_ref[j] = rows


def row_scales(g_ref):
    ones = jnp.ones((g_ref.shape[0], HEAD_WIDTH), f32)
    squares = tn(g_ref[:, 0, :], ones, lax.Precision.HIGHEST)
    inner = tn(g_ref[:, 1, :], ones, lax.Precision.HIGHEST)
    inverse = 1.0 / jnp.sqrt(squares / CHANNELS + EPSILON)
    return inverse, inverse * inner / CHANNELS


def backward_kernel(g_ref, att_ref, gh_ref, qh_ref, da_ref, bg_ref, inv_ref):
    inverse, mean = row_scales(g_ref)
    inv_ref[...] = inverse
    scaled = inverse * mean
    for h in range(att_ref.shape[0]):
        d = ((gh_ref[h] - att_ref[h] * scaled) * inverse).astype(bf16)
        da_ref[h] = d
        bg_ref[h] = tn(qh_ref[h], d).astype(bf16)


def softmax_kernel(pos_ref, sq_ref, kv0, kv1, kv2, kv3, out_hbm, out, ahead, sems):
    tokens, heads, width = out.shape
    kv = (kv0, kv1, kv2, kv3)
    scale = LOG2E * HEAD_WIDTH ** (-0.5)
    ones = jnp.ones((tokens, width), bf16)
    quarters = 4
    quarter = tokens // quarters

    def scores(chunk, rows, count):
        q = sq_ref[pl.ds(pl.multiple_of(chunk * rows, rows), rows), :]
        row = chunk * rows + lax.broadcasted_iota(jnp.int32, (rows, tokens), 0)
        column = lax.broadcasted_iota(jnp.int32, (rows, tokens), 1)
        own = jnp.where(column <= row // heads, nt(q, kv[0][0]), -1e30)
        return [own] + [nt(q, kv[b][0]) for b in range(1, count)]

    def weigh(parts, chunk, rows):
        top = None
        for s in parts:
            for j in range(0, tokens, 128):
                piece = s[:, j : j + 128]
                top = piece if top is None else jnp.maximum(top, piece)
        top = jnp.max(top, axis=1, keepdims=True) * scale
        total = None
        for b, s in enumerate(parts):
            p = jnp.exp2(s * scale - top).astype(bf16)
            o = nn(p, jnp.concatenate([kv[b][1], ones], axis=1))
            total = o if total is None else total + o
        chunk_tokens = rows // heads
        t0 = pl.multiple_of(chunk * chunk_tokens, chunk_tokens)
        out[pl.ds(t0, chunk_tokens)] = (
            (total[:, :width] / total[:, width:]).astype(bf16).reshape(chunk_tokens, heads, width)
        )

    def store(i):
        part = pl.ds(pl.multiple_of(i * quarter, quarter), quarter)
        return pltpu.make_async_copy(out.at[part], out_hbm.at[part], sems.at[i])

    def run(count):
        rows = 256
        per = quarter * heads // rows

        def body(i, carry):
            for j in range(per):
                chunk = i * per + j
                weigh(scores(chunk, rows, count), chunk, rows)
            store(i).start()
            return carry

        lax.fori_loop(0, quarters, body, 0)

    def run_ahead():
        rows = 512
        per = quarter * heads // rows
        last = quarters * per - 1

        def put(slot, chunk):
            for b, s in enumerate(scores(chunk, rows, WINDOW_BLOCKS)):
                ahead[slot, b] = s

        def body(i, carry):
            for j in range(per):
                chunk = i * per + j
                put((j + 1) % 2, jnp.minimum(chunk + 1, last))
                weigh([ahead[j % 2, b] for b in range(WINDOW_BLOCKS)], chunk, rows)
            store(i).start()
            return carry

        put(0, 0)
        lax.fori_loop(0, quarters, body, 0)

    have = pos_ref[0]
    for count in range(1, WINDOW_BLOCKS):
        pl.when(have == count - 1)(functools.partial(run, count))
    pl.when(have == WINDOW_BLOCKS - 1)(run_ahead)
    for i in range(quarters):
        store(i).wait()


def query_gradient_kernel(
    kh_ref, vh_ref, da_ref, pre_ref, att_ref, inv_ref, gain_ref, q2_ref,
    gq_hbm, norm_hbm, sq_ref, qs, ns, out, norm, sems,
):
    heads, tokens, width = kh_ref.shape
    half = tokens // 2
    below = causal_below(half)
    lo, hi = slice(0, half), slice(half, tokens)
    inverse = inv_ref[...]
    for h in range(heads):
        k, v, da = kh_ref[h], vh_ref[h], da_ref[h]
        d00 = jnp.where(below, nt(da[lo], v[lo]), 0.0).astype(bf16)
        d10 = nt(da[hi], v[lo]).astype(bf16)
        d11 = jnp.where(below, nt(da[hi], v[hi]), 0.0).astype(bf16)
        gq = nt(da, pre_ref[h])
        ns[pl.ds(h, tokens, stride=heads), :] = gain_ref[h : h + 1, :] * (att_ref[h] * inverse)
        qs[pl.ds(h, half, stride=heads), :] = gq[lo] + nn(d00, k[lo])
        qs[pl.ds(half * heads + h, half, stride=heads), :] = (
            gq[hi] + nn(d10, k[lo]) + nn(d11, k[hi])
        )
    pieces = sems.shape[0] // 2
    rows = tokens // pieces
    copies = []
    for i in range(pieces):
        part, flat = pl.ds(i * rows, rows), pl.ds(i * rows * heads, rows * heads)
        out[part] = qs[flat, :].astype(bf16).reshape(rows, heads, width)
        n = ns[flat, :].astype(bf16)
        norm[part] = n.reshape(rows, heads, width)
        copies += fetch(
            [(out.at[part], gq_hbm.at[part]), (norm.at[part], norm_hbm.at[part])],
            sems.at[pl.ds(2 * i, 2)],
        )
        q2 = q2_ref[part].astype(f32).reshape(rows * heads, width)
        sq_ref[flat, :] = (q2 + n.astype(f32)).astype(bf16)
    for copy in copies:
        copy.wait()


def key_value_local_kernel(qh_ref, kh_ref, vh_ref, da_ref, gk_ref, gv_ref):
    heads, tokens, width = qh_ref.shape
    half = tokens // 2
    r = lax.broadcasted_iota(jnp.int32, (half, half), 0)
    c = lax.broadcasted_iota(jnp.int32, (half, half), 1)
    above = r <= c
    lo, hi = slice(0, half), slice(half, tokens)

    def up(x):
        return jnp.where(above, x, 0.0).astype(bf16)

    def head(h):
        q, k, v, da = qh_ref[h], kh_ref[h], vh_ref[h], da_ref[h]
        for out, a, b, other in ((gk_ref, v, da, q), (gv_ref, k, q, da)):
            m00 = up(nt(a[lo], b[lo]))
            m01 = nt(a[lo], b[hi]).astype(bf16)
            m11 = up(nt(a[hi], b[hi]))
            out[h, :half] = nn(m00, other[lo]) + nn(m01, other[hi])
            out[h, half:] = nn(m11, other[hi])

    each(heads, head)


def finish_kernel(
    kh_ref, vh_ref, pk_ref, pv_ref, suf_ref, gk_hbm, gv_hbm, ks, vs, kb, vb, sems
):
    heads, tokens, width = kh_ref.shape
    pieces = sems.shape[0] // 2
    rows = tokens // pieces
    copies = []
    for i in range(pieces):
        part = pl.ds(i * rows, rows)
        for h in range(heads):
            suf = suf_ref[h]
            target = pl.ds(i * rows * heads + h, rows, stride=heads)
            ks[target, :] = pk_ref[h, part] + nt(vh_ref[h, part], suf)
            vs[target, :] = pv_ref[h, part] + nn(kh_ref[h, part], suf)
        flat = pl.ds(i * rows * heads, rows * heads)
        for src, buffer in ((ks, kb), (vs, vb)):
            buffer[part] = src[flat, :].astype(bf16).reshape(rows, heads, width)
        copies += fetch(
            [(kb.at[part], gk_hbm.at[part]), (vb.at[part], gv_hbm.at[part])],
            sems.at[pl.ds(2 * i, 2)],
        )
    for copy in copies:
        copy.wait()


def scan_kernel(back, recv_ref, *refs):
    *others, out_ref = refs
    count = recv_ref.shape[0]
    running = sum(other[...].astype(f32) for other in others)
    order = range(count) if back else range(count - 1, -1, -1)
    for i in order:
        out_ref[i] = running.astype(bf16)
        running = running + recv_ref[i].astype(f32)


def pair_kernel(own_ref, other_ref, out_ref):
    out_ref[...] = (own_ref[...].astype(f32) + other_ref[...].astype(f32)).astype(bf16)


def total_kernel(recv_ref, *refs):
    *sources, out_ref = refs[:3]
    for j, source in enumerate(sources):
        refs[3][j] = source[...]
    total = recv_ref[0].astype(f32)
    for i in range(1, recv_ref.shape[0]):
        total = total + recv_ref[i].astype(f32)
    out_ref[...] = total.astype(bf16)


def tied(*values):
    return lax.optimization_barrier(values)


def row_total(pieces):
    return call(total_kernel, [shape(pieces.shape[1:], bf16)], [pieces])[0]


def from_row(x, d, back):
    rows = lax.axis_size("y")
    return lax.ppermute(x, "y", [(i + d, i) if back else (i, i + d) for i in range(rows - d)])


def pair_total(own, other):
    return call(pair_kernel, [shape(own.shape, bf16)], [own, other])[0]


def scanned(pieces, totals, back):
    return call(
        functools.partial(scan_kernel, back), [shape(pieces.shape, bf16)], [pieces, *totals]
    )[0]


def spread(x):
    members = list(range(lax.axis_size("z")))[::-1]
    return lax.all_to_all(x, "z", 0, 0, tiled=True, axis_index_groups=[members])


def local(query, key, value, gain, cotangent, query2, key2, softmax_values):
    tokens, heads, width = query.shape
    flat = (tokens * heads, width)
    head_major = (heads, tokens, width)
    square = (heads, width, width)
    unit = 2 * tokens * tokens * width * heads
    ring = lax.axis_size(CTX)
    members = lax.axis_size(HEADS)
    token_buffer = pltpu.VMEM(query.shape, bf16)
    flat_buffer = pltpu.VMEM(flat, f32)

    def sems(n):
        return pltpu.SemaphoreType.DMA((n,))

    def onward(x):
        return lax.ppermute(x, CTX, [(i, i + 1) for i in range(ring - 1)])

    have = jnp.minimum(lax.axis_index(CTX), WINDOW_BLOCKS - 1).astype(jnp.int32).reshape(1)
    key, value, have = tied(key, value, have)

    kh, vh, states = call(
        state_kernel,
        [shape(head_major, bf16), shape(head_major, bf16), shape(square, bf16)],
        [key, value],
        [flat_buffer, flat_buffer],
        unit // 4,
    )
    states, query, cotangent = tied(states, query, cotangent)
    pieces, kh, vh = tied(spread(states), kh, vh)
    total, kv0 = call(
        total_kernel,
        [shape(square[1:], bf16), shape((2, tokens, width), bf16)],
        [pieces, key2[:, 0], softmax_values[:, 0]],
    )
    total, kh, vh = tied(total, kh, vh)
    kv1 = onward(kv0)
    totals = [from_row(total, d, False) for d in (1, 3, 2)]
    qh, gh, loc = call(
        local_kernel,
        [shape(head_major, bf16), shape(head_major, f32), shape(head_major, f32)],
        [query, cotangent, gain, kh, vh],
        [flat_buffer, flat_buffer],
        2 * unit,
    )
    *totals, kv1, loc = tied(*totals, kv1, loc)
    prefix, kv1 = tied(spread(scanned(pieces, totals, False)), kv1)
    kv2 = onward(kv1)
    att, part = call(
        attention_kernel,
        [shape(head_major, f32), shape((members, 2, tokens), f32)],
        [loc, qh, gh, prefix],
        (),
        unit // 4,
    )
    gathered = lax.all_to_all(part, HEADS, 0, 0, tiled=True)
    gathered, kv2 = tied(gathered, kv2)
    da, block_grad, inverse = call(
        backward_kernel,
        [shape(head_major, bf16), shape(square, bf16), shape((tokens, width), f32)],
        [gathered, att, gh, qh],
        (),
        unit // 4,
    )
    back_pieces, att, da, inverse, kv2 = tied(spread(block_grad), att, da, inverse, kv2)
    kv3 = onward(kv2)
    gq, normed, sq = call(
        query_gradient_kernel,
        [shape(query.shape, bf16), shape(query.shape, bf16), shape(flat, bf16)],
        [kh, vh, da, prefix, att, inverse, gain, query2],
        [flat_buffer, flat_buffer, token_buffer, token_buffer, sems(8)],
        2 * unit,
        hbm_out=(0, 1),
    )
    back_total, gq, da = tied(row_total(back_pieces), gq, da)
    back_near = from_row(back_total, 1, True)
    pk, pv = call(
        key_value_local_kernel, [shape(head_major, f32)] * 2, [qh, kh, vh, da], (), 4 * unit
    )
    back_near, pk, pv, sq = tied(back_near, pk, pv, sq)
    back_far = from_row(pair_total(back_total, back_near), 2, True)
    (attended,) = call(
        softmax_kernel,
        [shape(query.shape, bf16)],
        [have, sq, kv0, kv1, kv2, kv3],
        [token_buffer, pltpu.VMEM((2, WINDOW_BLOCKS, tokens, tokens), f32), sems(4)],
        8 * unit,
        smem_first=True,
        vmem=40,
        hbm_out=(0,),
    )
    back_far, normed, attended, gq = tied(back_far, normed, attended, gq)
    suffix = spread(scanned(back_pieces, [back_near, back_far], True))
    gk, gv = call(
        finish_kernel,
        [shape(query.shape, bf16)] * 2,
        [kh, vh, pk, pv, suffix],
        [flat_buffer, flat_buffer, token_buffer, token_buffer, sems(8)],
        unit // 2,
        hbm_out=(0, 1),
    )
    return normed, gq, gk, gv, attended


def solution(mesh):
    sizes = (4, 8, 4, 2)
    fine = Mesh(mesh.devices.reshape(sizes), ("y", "z", "x", "core"))
    tokens = P(CTX, HEADS, None)
    return jax.shard_map(
        local,
        mesh=fine,
        in_specs=(tokens, tokens, tokens, P(HEADS, None), tokens, tokens, tokens, tokens),
        out_specs=(tokens,) * 5,
        check_vma=False,
    )
```

```python
import functools
import jax
import jax.numpy as jnp
from jax import lax
from jax.experimental import pallas as pl
from jax.experimental.pallas import tpu as pltpu
from jax.sharding import Mesh, PartitionSpec as P

ATTN_HEADS = 64
HEAD_WIDTH = 128
WINDOW_BLOCKS = 4
CHANNELS = ATTN_HEADS * HEAD_WIDTH
EPSILON = 1e-06
LOG2E = 1.4426950408889634

f32 = jnp.float32
bf16 = jnp.bfloat16
MIB = 1 << 20
HEADS = ("x", "core")
CTX = ("y", "z")


def nn(a, b, precision=None):
    return lax.dot_general(
        a, b, (((1,), (0,)), ((), ())), precision=precision, preferred_element_type=f32
    )


def nt(a, b, precision=None):
    return lax.dot_general(
        a, b, (((1,), (1,)), ((), ())), precision=precision, preferred_element_type=f32
    )


def tn(a, b, precision=None):
    return lax.dot_general(
        a, b, (((0,), (0,)), ((), ())), precision=precision, preferred_element_type=f32
    )


def call(kernel, out_shapes, args, scratch=(), flops=0, smem_first=False, vmem=20, hbm_in=(), hbm_out=()):
    def place(i, far):
        return pl.BlockSpec(memory_space=pltpu.HBM if i in far else pltpu.VMEM)

    specs = [place(i, hbm_in) for i in range(len(args))]
    if smem_first:
        specs[0] = pl.BlockSpec(memory_space=pltpu.SMEM)
    moved = sum(a.size * a.dtype.itemsize for a in (*args, *out_shapes))
    return pl.pallas_call(
        kernel,
        out_shape=out_shapes,
        in_specs=specs,
        out_specs=[place(i, hbm_out) for i in range(len(out_shapes))],
        scratch_shapes=list(scratch),
        compiler_params=pltpu.CompilerParams(vmem_limit_bytes=vmem * MIB),
        cost_estimate=pl.CostEstimate(flops=flops, bytes_accessed=moved, transcendentals=0),
    )(*args)


def shape(dims, dtype):
    return jax.ShapeDtypeStruct(dims, dtype)


def fetch(pairs, sems):
    copies = []
    for i, (src, dst) in enumerate(pairs):
        copy = pltpu.make_async_copy(src, dst, sems.at[i])
        copy.start()
        copies.append(copy)
    return copies


def state_kernel(k_ref, v_ref, kh_ref, vh_ref, st_ref, ks, vs):
    tokens, heads, width = k_ref.shape
    ks[...] = k_ref[...].astype(f32).reshape(tokens * heads, width)
    vs[...] = v_ref[...].astype(f32).reshape(tokens * heads, width)
    for h in range(heads):
        kh = ks[pl.ds(h, tokens, stride=heads), :].astype(bf16)
        vh = vs[pl.ds(h, tokens, stride=heads), :].astype(bf16)
        kh_ref[h] = kh
        vh_ref[h] = vh
        st_ref[h] = tn(kh, vh).astype(bf16)


def each(count, body, unroll=8):
    def step(i, carry):
        body(i)
        return carry

    lax.fori_loop(0, count, step, 0, unroll=unroll)


def causal_below(rows):
    r = lax.broadcasted_iota(jnp.int32, (rows, rows), 0)
    c = lax.broadcasted_iota(jnp.int32, (rows, rows), 1)
    return c <= r


def local_kernel(q_ref, c_ref, gain_ref, kh_ref, vh_ref, qh_ref, gh_ref, loc_ref, qs, cs):
    tokens, heads, width = q_ref.shape
    half = tokens // 2
    qs[...] = q_ref[...].astype(f32).reshape(tokens * heads, width)
    cs[...] = (c_ref[...].astype(f32) * gain_ref[...][None]).reshape(tokens * heads, width)
    causal = causal_below(half)

    def head(h):
        qh = qs[pl.ds(h, tokens, stride=heads), :].astype(bf16)
        qh_ref[h] = qh
        gh_ref[h] = cs[pl.ds(h, tokens, stride=heads), :]
        kh = kh_ref[h]
        vh = vh_ref[h]
        w0 = jnp.where(causal, nt(qh[:half], kh[:half]), 0.0).astype(bf16)
        w10 = nt(qh[half:], kh[:half]).astype(bf16)
        w11 = jnp.where(causal, nt(qh[half:], kh[half:]), 0.0).astype(bf16)
        loc_ref[h, :half] = nn(w0, vh[:half])
        loc_ref[h, half:] = nn(w10, vh[:half]) + nn(w11, vh[half:])

    each(heads, head)


def attention_kernel(loc_ref, qh_ref, gh_ref, pre_ref, att_ref, part_ref):
    heads, tokens, width = loc_ref.shape
    squares = jnp.zeros((tokens, width), f32)
    inner = jnp.zeros((tokens, width), f32)
    for h in range(heads):
        att = loc_ref[h] + nn(qh_ref[h], pre_ref[h])
        att_ref[h] = att
        squares = squares + att * att
        inner = inner + att * gh_ref[h]
    ones = jnp.ones((8, width), f32)
    rows = jnp.concatenate(
        [
            nt(ones, squares, lax.Precision.HIGHEST)[0:1],
            nt(ones, inner, lax.Precision.HIGHEST)[0:1],
        ]
    )
    for j in range(part_ref.shape[0]):
        part_ref[j] = rows


def row_scales(g_ref):
    ones = jnp.ones((g_ref.shape[0], HEAD_WIDTH), f32)
    squares = tn(g_ref[:, 0, :], ones, lax.Precision.HIGHEST)
    inner = tn(g_ref[:, 1, :], ones, lax.Precision.HIGHEST)
    inverse = 1.0 / jnp.sqrt(squares / CHANNELS + EPSILON)
    return inverse, inverse * inner / CHANNELS


def backward_kernel(g_ref, att_ref, gh_ref, qh_ref, da_ref, bg_ref, inv_ref):
    inverse, mean = row_scales(g_ref)
    inv_ref[...] = inverse
    scaled = inverse * mean
    for h in range(att_ref.shape[0]):
        d = ((gh_ref[h] - att_ref[h] * scaled) * inverse).astype(bf16)
        da_ref[h] = d
        bg_ref[h] = tn(qh_ref[h], d).astype(bf16)


def final_kernel(
    pos_ref, sq_ref, kv0, kv1, kv2, kv3,
    kh_ref, vh_ref, pk_ref, pv_ref, suf_ref, gq_ref, norm_ref,
    norm_hbm, gq_hbm, gk_hbm, gv_hbm, out_hbm,
    out, ahead, ks, vs, kb, vb, sems, done_sems, grad_sems,
):
    tokens, heads, width = out.shape
    kv = (kv0, kv1, kv2, kv3)
    copies = fetch([(norm_ref, norm_hbm), (gq_ref, gq_hbm)], done_sems)
    pieces = grad_sems.shape[0]
    rows = tokens // pieces
    for i in range(pieces):
        part, flat = pl.ds(i * rows, rows), pl.ds(i * rows * heads, rows * heads)
        for h in range(heads):
            suf = suf_ref[h]
            target = pl.ds(i * rows * heads + h, rows, stride=heads)
            ks[target, :] = pk_ref[h, part].astype(f32) + nt(vh_ref[h, part], suf)
            vs[target, :] = pv_ref[h, part].astype(f32) + nn(kh_ref[h, part], suf)
        for src, buffer in ((ks, kb), (vs, vb)):
            buffer[part] = src[flat, :].astype(bf16).reshape(rows, heads, width)
        copies += fetch(
            [(kb.at[part], gk_hbm.at[part]), (vb.at[part], gv_hbm.at[part])], grad_sems.at[i]
        )
    scale = LOG2E * HEAD_WIDTH ** (-0.5)
    ones = jnp.ones((tokens, width), bf16)
    quarters = 4
    quarter = tokens // quarters

    def scores(chunk, rows, count):
        q = sq_ref[pl.ds(pl.multiple_of(chunk * rows, rows), rows), :]
        row = chunk * rows + lax.broadcasted_iota(jnp.int32, (rows, tokens), 0)
        column = lax.broadcasted_iota(jnp.int32, (rows, tokens), 1)
        own = jnp.where(column <= row // heads, nt(q, kv[0][0]), -1e30)
        return [own] + [nt(q, kv[b][0]) for b in range(1, count)]

    def weigh(parts, chunk, rows):
        top = None
        for s in parts:
            for j in range(0, tokens, 128):
                piece = s[:, j : j + 128]
                top = piece if top is None else jnp.maximum(top, piece)
        top = jnp.max(top, axis=1, keepdims=True) * scale
        total = None
        for b, s in enumerate(parts):
            p = jnp.exp2(s * scale - top).astype(bf16)
            o = nn(p, jnp.concatenate([kv[b][1], ones], axis=1))
            total = o if total is None else total + o
        chunk_tokens = rows // heads
        t0 = pl.multiple_of(chunk * chunk_tokens, chunk_tokens)
        out[pl.ds(t0, chunk_tokens)] = (
            (total[:, :width] / total[:, width:]).astype(bf16).reshape(chunk_tokens, heads, width)
        )

    def store(i):
        part = pl.ds(pl.multiple_of(i * quarter, quarter), quarter)
        return pltpu.make_async_copy(out.at[part], out_hbm.at[part], sems.at[i])

    def run(count):
        rows = 256
        per = quarter * heads // rows

        def body(i, carry):
            for j in range(per):
                chunk = i * per + j
                weigh(scores(chunk, rows, count), chunk, rows)
            store(i).start()
            return carry

        lax.fori_loop(0, quarters, body, 0)

    def run_ahead():
        rows = 512
        per = quarter * heads // rows
        last = quarters * per - 1

        def put(slot, chunk):
            for b, s in enumerate(scores(chunk, rows, WINDOW_BLOCKS)):
                ahead[slot, b] = s

        def body(i, carry):
            for j in range(per):
                chunk = i * per + j
                put((j + 1) % 2, jnp.minimum(chunk + 1, last))
                weigh([ahead[j % 2, b] for b in range(WINDOW_BLOCKS)], chunk, rows)
            store(i).start()
            return carry

        put(0, 0)
        lax.fori_loop(0, quarters, body, 0)

    have = pos_ref[0]
    for count in range(1, WINDOW_BLOCKS):
        pl.when(have == count - 1)(functools.partial(run, count))
    pl.when(have == WINDOW_BLOCKS - 1)(run_ahead)
    for i in range(quarters):
        store(i).wait()
    for copy in copies:
        copy.wait()


def query_gradient_kernel(
    kh_ref, vh_ref, da_ref, pre_ref, att_ref, inv_ref, gain_ref, q2_ref,
    gq_ref, norm_ref, sq_ref, qs, ns,
):
    heads, tokens, width = kh_ref.shape
    half = tokens // 2
    below = causal_below(half)
    lo, hi = slice(0, half), slice(half, tokens)
    inverse = inv_ref[...]
    for h in range(heads):
        k, v, da = kh_ref[h], vh_ref[h], da_ref[h]
        d00 = jnp.where(below, nt(da[lo], v[lo]), 0.0).astype(bf16)
        d10 = nt(da[hi], v[lo]).astype(bf16)
        d11 = jnp.where(below, nt(da[hi], v[hi]), 0.0).astype(bf16)
        gq = nt(da, pre_ref[h])
        ns[pl.ds(h, tokens, stride=heads), :] = gain_ref[h : h + 1, :] * (att_ref[h] * inverse)
        qs[pl.ds(h, half, stride=heads), :] = gq[lo] + nn(d00, k[lo])
        qs[pl.ds(half * heads + h, half, stride=heads), :] = (
            gq[hi] + nn(d10, k[lo]) + nn(d11, k[hi])
        )
    gq_ref[...] = qs[...].astype(bf16).reshape(tokens, heads, width)
    n = ns[...].astype(bf16)
    norm_ref[...] = n.reshape(tokens, heads, width)
    q2 = q2_ref[...].astype(f32).reshape(tokens * heads, width)
    sq_ref[...] = (q2 + n.astype(f32)).astype(bf16)


def key_value_local_kernel(qh_ref, kh_ref, vh_ref, da_ref, gk_ref, gv_ref):
    heads, tokens, width = qh_ref.shape
    half = tokens // 2
    r = lax.broadcasted_iota(jnp.int32, (half, half), 0)
    c = lax.broadcasted_iota(jnp.int32, (half, half), 1)
    above = r <= c
    lo, hi = slice(0, half), slice(half, tokens)

    def up(x):
        return jnp.where(above, x, 0.0).astype(bf16)

    def head(h):
        q, k, v, da = qh_ref[h], kh_ref[h], vh_ref[h], da_ref[h]
        for out, a, b, other in ((gk_ref, v, da, q), (gv_ref, k, q, da)):
            m00 = up(nt(a[lo], b[lo]))
            m01 = nt(a[lo], b[hi]).astype(bf16)
            m11 = up(nt(a[hi], b[hi]))
            out[h, :half] = (nn(m00, other[lo]) + nn(m01, other[hi])).astype(bf16)
            out[h, half:] = nn(m11, other[hi]).astype(bf16)

    each(heads, head)


def scan_kernel(back, recv_ref, *refs):
    *others, out_ref = refs
    count = recv_ref.shape[0]
    running = sum(other[...].astype(f32) for other in others)
    order = range(count) if back else range(count - 1, -1, -1)
    for i in order:
        out_ref[i] = running.astype(bf16)
        running = running + recv_ref[i].astype(f32)


def pair_kernel(own_ref, other_ref, out_ref):
    out_ref[...] = (own_ref[...].astype(f32) + other_ref[...].astype(f32)).astype(bf16)


def total_kernel(recv_ref, *refs):
    *sources, out_ref = refs[:3]
    for j, source in enumerate(sources):
        refs[3][j] = source[...]
    total = recv_ref[0].astype(f32)
    for i in range(1, recv_ref.shape[0]):
        total = total + recv_ref[i].astype(f32)
    out_ref[...] = total.astype(bf16)


def tied(*values):
    return lax.optimization_barrier(values)


def row_total(pieces):
    return call(total_kernel, [shape(pieces.shape[1:], bf16)], [pieces])[0]


def from_row(x, d, back):
    rows = lax.axis_size("y")
    return lax.ppermute(x, "y", [(i + d, i) if back else (i, i + d) for i in range(rows - d)])


def pair_total(own, other):
    return call(pair_kernel, [shape(own.shape, bf16)], [own, other])[0]


def scanned(pieces, totals, back):
    return call(
        functools.partial(scan_kernel, back), [shape(pieces.shape, bf16)], [pieces, *totals]
    )[0]


def spread(x):
    members = list(range(lax.axis_size("z")))[::-1]
    return lax.all_to_all(x, "z", 0, 0, tiled=True, axis_index_groups=[members])


def local(query, key, value, gain, cotangent, query2, key2, softmax_values):
    tokens, heads, width = query.shape
    flat = (tokens * heads, width)
    head_major = (heads, tokens, width)
    square = (heads, width, width)
    unit = 2 * tokens * tokens * width * heads
    ring = lax.axis_size(CTX)
    members = lax.axis_size(HEADS)
    token_buffer = pltpu.VMEM(query.shape, bf16)
    flat_buffer = pltpu.VMEM(flat, f32)

    def sems(n):
        return pltpu.SemaphoreType.DMA((n,))

    def onward(x):
        return lax.ppermute(x, CTX, [(i, i + 1) for i in range(ring - 1)])

    have = jnp.minimum(lax.axis_index(CTX), WINDOW_BLOCKS - 1).astype(jnp.int32).reshape(1)
    key, value, have = tied(key, value, have)

    kh, vh, states = call(
        state_kernel,
        [shape(head_major, bf16), shape(head_major, bf16), shape(square, bf16)],
        [key, value],
        [flat_buffer, flat_buffer],
        unit // 4,
    )
    states, query, cotangent = tied(states, query, cotangent)
    pieces, kh, vh = tied(spread(states), kh, vh)
    total, kv0 = call(
        total_kernel,
        [shape(square[1:], bf16), shape((2, tokens, width), bf16)],
        [pieces, key2[:, 0], softmax_values[:, 0]],
    )
    total, kh, vh = tied(total, kh, vh)
    kv1 = onward(kv0)
    totals = [from_row(total, d, False) for d in (1, 3, 2)]
    qh, gh, loc = call(
        local_kernel,
        [shape(head_major, bf16), shape(head_major, f32), shape(head_major, f32)],
        [query, cotangent, gain, kh, vh],
        [flat_buffer, flat_buffer],
        2 * unit,
    )
    *totals, kv1, loc = tied(*totals, kv1, loc)
    prefix, kv1 = tied(spread(scanned(pieces, totals, False)), kv1)
    kv2 = onward(kv1)
    att, part = call(
        attention_kernel,
        [shape(head_major, f32), shape((members, 2, tokens), f32)],
        [loc, qh, gh, prefix],
        (),
        unit // 4,
    )
    gathered = lax.all_to_all(part, HEADS, 0, 0, tiled=True)
    gathered, kv2 = tied(gathered, kv2)
    da, block_grad, inverse = call(
        backward_kernel,
        [shape(head_major, bf16), shape(square, bf16), shape((tokens, width), f32)],
        [gathered, att, gh, qh],
        (),
        unit // 4,
    )
    back_pieces, att, da, inverse, kv2 = tied(spread(block_grad), att, da, inverse, kv2)
    kv3 = onward(kv2)
    back_total = row_total(back_pieces)
    back_near = from_row(back_total, 1, True)
    gq, normed, sq = call(
        query_gradient_kernel,
        [shape(query.shape, bf16), shape(query.shape, bf16), shape(flat, bf16)],
        [kh, vh, da, prefix, att, inverse, gain, query2],
        [flat_buffer, flat_buffer],
        2 * unit,
    )
    back_near, gq, da = tied(back_near, gq, da)
    back_far = from_row(pair_total(back_total, back_near), 2, True)
    pk, pv = call(
        key_value_local_kernel, [shape(head_major, bf16)] * 2, [qh, kh, vh, da], (), 4 * unit
    )
    back_far, pk, sq, kv3 = tied(back_far, pk, sq, kv3)
    suffix, sq = tied(spread(scanned(back_pieces, [back_near, back_far], True)), sq)
    normed, gq, gk, gv, attended = call(
        final_kernel,
        [shape(query.shape, bf16)] * 5,
        [have, sq, kv0, kv1, kv2, kv3, kh, vh, pk, pv, suffix, gq, normed],
        [
            token_buffer,
            pltpu.VMEM((2, WINDOW_BLOCKS, tokens, tokens), f32),
            flat_buffer,
            flat_buffer,
            token_buffer,
            token_buffer,
            sems(4),
            sems(2),
            pltpu.SemaphoreType.DMA((4, 2)),
        ],
        9 * unit,
        smem_first=True,
        vmem=32,
        hbm_out=range(5),
    )
    return normed, gq, gk, gv, attended


def solution(mesh):
    sizes = (4, 8, 4, 2)
    fine = Mesh(mesh.devices.reshape(sizes), ("y", "z", "x", "core"))
    tokens = P(CTX, HEADS, None)
    return jax.shard_map(
        local,
        mesh=fine,
        in_specs=(tokens, tokens, tokens, P(HEADS, None), tokens, tokens, tokens, tokens),
        out_specs=(tokens,) * 5,
        check_vma=False,
    )
```

```python
import functools
import jax
import jax.numpy as jnp
from jax import lax
from jax.experimental import pallas as pl
from jax.experimental.pallas import tpu as pltpu
from jax.sharding import Mesh, PartitionSpec as P

ATTN_HEADS = 64
HEAD_WIDTH = 128
WINDOW_BLOCKS = 4
CHANNELS = ATTN_HEADS * HEAD_WIDTH
EPSILON = 1e-06
LOG2E = 1.4426950408889634

f32 = jnp.float32
bf16 = jnp.bfloat16
MIB = 1 << 20
HEADS = ("x", "core")
CTX = ("y", "z")


def nn(a, b, precision=None):
    return lax.dot_general(
        a, b, (((1,), (0,)), ((), ())), precision=precision, preferred_element_type=f32
    )


def nt(a, b, precision=None):
    return lax.dot_general(
        a, b, (((1,), (1,)), ((), ())), precision=precision, preferred_element_type=f32
    )


def tn(a, b, precision=None):
    return lax.dot_general(
        a, b, (((0,), (0,)), ((), ())), precision=precision, preferred_element_type=f32
    )


def call(kernel, out_shapes, args, scratch=(), flops=0, smem_first=False, vmem=20, hbm_in=(), hbm_out=()):
    def place(i, far):
        return pl.BlockSpec(memory_space=pltpu.HBM if i in far else pltpu.VMEM)

    specs = [place(i, hbm_in) for i in range(len(args))]
    if smem_first:
        specs[0] = pl.BlockSpec(memory_space=pltpu.SMEM)
    moved = sum(a.size * a.dtype.itemsize for a in (*args, *out_shapes))
    return pl.pallas_call(
        kernel,
        out_shape=out_shapes,
        in_specs=specs,
        out_specs=[place(i, hbm_out) for i in range(len(out_shapes))],
        scratch_shapes=list(scratch),
        compiler_params=pltpu.CompilerParams(vmem_limit_bytes=vmem * MIB),
        cost_estimate=pl.CostEstimate(flops=flops, bytes_accessed=moved, transcendentals=0),
    )(*args)


def shape(dims, dtype):
    return jax.ShapeDtypeStruct(dims, dtype)


def fetch(pairs, sems):
    copies = []
    for i, (src, dst) in enumerate(pairs):
        copy = pltpu.make_async_copy(src, dst, sems.at[i])
        copy.start()
        copies.append(copy)
    return copies


def head_major_kernel(x_ref, out_ref, flat):
    tokens, heads, width = x_ref.shape
    flat[...] = x_ref[...].astype(f32).reshape(tokens * heads, width)
    for h in range(heads):
        out_ref[h] = flat[pl.ds(h, tokens, stride=heads), :].astype(bf16)


def state_kernel(kh_ref, v_ref, vh_ref, st_ref, vs):
    tokens, heads, width = v_ref.shape
    vs[...] = v_ref[...].astype(f32).reshape(tokens * heads, width)
    for h in range(heads):
        vh = vs[pl.ds(h, tokens, stride=heads), :].astype(bf16)
        vh_ref[h] = vh
        st_ref[h] = tn(kh_ref[h], vh).astype(bf16)


def each(count, body, unroll=8):
    def step(i, carry):
        body(i)
        return carry

    lax.fori_loop(0, count, step, 0, unroll=unroll)


def causal_below(rows):
    r = lax.broadcasted_iota(jnp.int32, (rows, rows), 0)
    c = lax.broadcasted_iota(jnp.int32, (rows, rows), 1)
    return c <= r


def local_kernel(q_ref, c_ref, gain_ref, kh_ref, vh_ref, qh_ref, gh_ref, loc_ref, qs, cs):
    tokens, heads, width = q_ref.shape
    half = tokens // 2
    qs[...] = q_ref[...].astype(f32).reshape(tokens * heads, width)
    cs[...] = (c_ref[...].astype(f32) * gain_ref[...][None]).reshape(tokens * heads, width)
    causal = causal_below(half)

    def head(h):
        qh = qs[pl.ds(h, tokens, stride=heads), :].astype(bf16)
        qh_ref[h] = qh
        gh_ref[h] = cs[pl.ds(h, tokens, stride=heads), :]
        kh = kh_ref[h]
        vh = vh_ref[h]
        w0 = jnp.where(causal, nt(qh[:half], kh[:half]), 0.0).astype(bf16)
        w10 = nt(qh[half:], kh[:half]).astype(bf16)
        w11 = jnp.where(causal, nt(qh[half:], kh[half:]), 0.0).astype(bf16)
        loc_ref[h, :half] = nn(w0, vh[:half])
        loc_ref[h, half:] = nn(w10, vh[:half]) + nn(w11, vh[half:])

    each(heads, head)


def terms(x):
    parts = []
    for _ in range(3):
        high = x.astype(bf16)
        parts.append(high)
        x = x - high.astype(f32)
    return parts


def attention_kernel(loc_ref, qh_ref, gh_ref, pre_ref, att_ref, part_ref):
    heads, tokens, width = loc_ref.shape
    squares = jnp.zeros((tokens, width), f32)
    inner = jnp.zeros((tokens, width), f32)
    for h in range(heads):
        att = loc_ref[h] + nn(qh_ref[h], pre_ref[h])
        att_ref[h] = att
        squares = squares + att * att
        inner = inner + att * gh_ref[h]
    ones = jnp.ones((8, width), bf16)
    rows = jnp.concatenate(
        [sum(nt(ones, part) for part in terms(x))[0:1] for x in (squares, inner)]
    )
    for j in range(part_ref.shape[0]):
        part_ref[j] = rows


def row_scales(g_ref):
    ones = jnp.ones((g_ref.shape[0], HEAD_WIDTH), bf16)
    squares = sum(tn(part, ones) for part in terms(g_ref[:, 0, :]))
    inner = sum(tn(part, ones) for part in terms(g_ref[:, 1, :]))
    inverse = 1.0 / jnp.sqrt(squares / CHANNELS + EPSILON)
    return inverse, inverse * inner / CHANNELS


def backward_kernel(g_ref, att_ref, gh_ref, qh_ref, da_ref, bg_ref, inv_ref):
    inverse, mean = row_scales(g_ref)
    inv_ref[...] = inverse
    scaled = inverse * mean
    for h in range(att_ref.shape[0]):
        d = ((gh_ref[h] - att_ref[h] * scaled) * inverse).astype(bf16)
        da_ref[h] = d
        bg_ref[h] = tn(qh_ref[h], d).astype(bf16)


def final_kernel(
    pos_ref, sq_ref, kv0, kv1, kv2, kv3,
    kh_ref, vh_ref, pk_ref, pv_ref, suf_ref, gq_ref, norm_ref,
    norm_hbm, gq_hbm, gk_hbm, gv_hbm, out_hbm,
    out, ahead, ks, vs, kb, vb, sems, done_sems, grad_sems,
):
    tokens, heads, width = out.shape
    kv = (kv0, kv1, kv2, kv3)
    copies = fetch([(norm_ref, norm_hbm), (gq_ref, gq_hbm)], done_sems)
    pieces = grad_sems.shape[0]
    rows = tokens // pieces
    for i in range(pieces):
        part, flat = pl.ds(i * rows, rows), pl.ds(i * rows * heads, rows * heads)
        for h in range(heads):
            suf = suf_ref[h]
            target = pl.ds(i * rows * heads + h, rows, stride=heads)
            ks[target, :] = pk_ref[h, part].astype(f32) + nt(vh_ref[h, part], suf)
            vs[target, :] = pv_ref[h, part].astype(f32) + nn(kh_ref[h, part], suf)
        for src, buffer in ((ks, kb), (vs, vb)):
            buffer[part] = src[flat, :].astype(bf16).reshape(rows, heads, width)
        copies += fetch(
            [(kb.at[part], gk_hbm.at[part]), (vb.at[part], gv_hbm.at[part])], grad_sems.at[i]
        )
    scale = LOG2E * HEAD_WIDTH ** (-0.5)
    ones = jnp.ones((tokens, width), bf16)
    quarters = 4
    quarter = tokens // quarters

    def scores(chunk, rows, count):
        q = sq_ref[pl.ds(pl.multiple_of(chunk * rows, rows), rows), :]
        row = chunk * rows + lax.broadcasted_iota(jnp.int32, (rows, tokens), 0)
        column = lax.broadcasted_iota(jnp.int32, (rows, tokens), 1)
        own = jnp.where(column <= row // heads, nt(q, kv[0][0]), -1e30)
        return [own] + [nt(q, kv[b][0]) for b in range(1, count)]

    def weigh(parts, chunk, rows):
        top = None
        for s in parts:
            for j in range(0, tokens, 128):
                piece = s[:, j : j + 128]
                top = piece if top is None else jnp.maximum(top, piece)
        top = jnp.max(top, axis=1, keepdims=True) * scale
        total = None
        for b, s in enumerate(parts):
            p = jnp.exp2(s * scale - top).astype(bf16)
            o = nn(p, jnp.concatenate([kv[b][1], ones], axis=1))
            total = o if total is None else total + o
        chunk_tokens = rows // heads
        t0 = pl.multiple_of(chunk * chunk_tokens, chunk_tokens)
        out[pl.ds(t0, chunk_tokens)] = (
            (total[:, :width] / total[:, width:]).astype(bf16).reshape(chunk_tokens, heads, width)
        )

    def store(i):
        part = pl.ds(pl.multiple_of(i * quarter, quarter), quarter)
        return pltpu.make_async_copy(out.at[part], out_hbm.at[part], sems.at[i])

    def run(count):
        rows = 256
        per = quarter * heads // rows

        def body(i, carry):
            for j in range(per):
                chunk = i * per + j
                weigh(scores(chunk, rows, count), chunk, rows)
            store(i).start()
            return carry

        lax.fori_loop(0, quarters, body, 0)

    def run_ahead():
        rows = 512
        per = quarter * heads // rows
        last = quarters * per - 1

        def put(slot, chunk):
            for b, s in enumerate(scores(chunk, rows, WINDOW_BLOCKS)):
                ahead[slot, b] = s

        def body(i, carry):
            for j in range(per):
                chunk = i * per + j
                put((j + 1) % 2, jnp.minimum(chunk + 1, last))
                weigh([ahead[j % 2, b] for b in range(WINDOW_BLOCKS)], chunk, rows)
            store(i).start()
            return carry

        put(0, 0)
        lax.fori_loop(0, quarters, body, 0)

    have = pos_ref[0]
    for count in range(1, WINDOW_BLOCKS):
        pl.when(have == count - 1)(functools.partial(run, count))
    pl.when(have == WINDOW_BLOCKS - 1)(run_ahead)
    for i in range(quarters):
        store(i).wait()
    for copy in copies:
        copy.wait()


def query_gradient_kernel(
    kh_ref, vh_ref, da_ref, pre_ref, att_ref, inv_ref, gain_ref, q2_ref,
    gq_ref, norm_ref, sq_ref, qs, ns,
):
    heads, tokens, width = kh_ref.shape
    half = tokens // 2
    below = causal_below(half)
    lo, hi = slice(0, half), slice(half, tokens)
    inverse = inv_ref[...]
    for h in range(heads):
        k, v, da = kh_ref[h], vh_ref[h], da_ref[h]
        d00 = jnp.where(below, nt(da[lo], v[lo]), 0.0).astype(bf16)
        d10 = nt(da[hi], v[lo]).astype(bf16)
        d11 = jnp.where(below, nt(da[hi], v[hi]), 0.0).astype(bf16)
        gq = nt(da, pre_ref[h])
        ns[pl.ds(h, tokens, stride=heads), :] = gain_ref[h : h + 1, :] * (att_ref[h] * inverse)
        qs[pl.ds(h, half, stride=heads), :] = gq[lo] + nn(d00, k[lo])
        qs[pl.ds(half * heads + h, half, stride=heads), :] = (
            gq[hi] + nn(d10, k[lo]) + nn(d11, k[hi])
        )
    gq_ref[...] = qs[...].astype(bf16).reshape(tokens, heads, width)
    n = ns[...].astype(bf16)
    norm_ref[...] = n.reshape(tokens, heads, width)
    q2 = q2_ref[...].astype(f32).reshape(tokens * heads, width)
    sq_ref[...] = (q2 + n.astype(f32)).astype(bf16)


def key_value_local_kernel(qh_ref, kh_ref, vh_ref, da_ref, gk_ref, gv_ref):
    heads, tokens, width = qh_ref.shape
    half = tokens // 2
    r = lax.broadcasted_iota(jnp.int32, (half, half), 0)
    c = lax.broadcasted_iota(jnp.int32, (half, half), 1)
    above = r <= c
    lo, hi = slice(0, half), slice(half, tokens)

    def up(x):
        return jnp.where(above, x, 0.0).astype(bf16)

    def head(h):
        q, k, v, da = qh_ref[h], kh_ref[h], vh_ref[h], da_ref[h]
        for out, a, b, other in ((gk_ref, v, da, q), (gv_ref, k, q, da)):
            m00 = up(nt(a[lo], b[lo]))
            m01 = nt(a[lo], b[hi]).astype(bf16)
            m11 = up(nt(a[hi], b[hi]))
            out[h, :half] = (nn(m00, other[lo]) + nn(m01, other[hi])).astype(bf16)
            out[h, half:] = nn(m11, other[hi]).astype(bf16)

    each(heads, head)


def scan_kernel(back, recv_ref, *refs):
    *others, out_ref = refs
    count = recv_ref.shape[0]
    running = sum(other[...].astype(f32) for other in others)
    order = range(count) if back else range(count - 1, -1, -1)
    for i in order:
        out_ref[i] = running.astype(bf16)
        running = running + recv_ref[i].astype(f32)


def pair_kernel(own_ref, other_ref, out_ref):
    out_ref[...] = (own_ref[...].astype(f32) + other_ref[...].astype(f32)).astype(bf16)


def total_kernel(recv_ref, *refs):
    *sources, out_ref = refs[:3]
    for j, source in enumerate(sources):
        refs[3][j] = source[...]
    total = recv_ref[0].astype(f32)
    for i in range(1, recv_ref.shape[0]):
        total = total + recv_ref[i].astype(f32)
    out_ref[...] = total.astype(bf16)


def tied(*values):
    return lax.optimization_barrier(values)


def row_total(pieces):
    return call(total_kernel, [shape(pieces.shape[1:], bf16)], [pieces])[0]


def from_row(x, d, back):
    rows = lax.axis_size("y")
    return lax.ppermute(x, "y", [(i + d, i) if back else (i, i + d) for i in range(rows - d)])


def pair_total(own, other):
    return call(pair_kernel, [shape(own.shape, bf16)], [own, other])[0]


def scanned(pieces, totals, back):
    return call(
        functools.partial(scan_kernel, back), [shape(pieces.shape, bf16)], [pieces, *totals]
    )[0]


def spread(x):
    members = list(range(lax.axis_size("z")))[::-1]
    return lax.all_to_all(x, "z", 0, 0, tiled=True, axis_index_groups=[members])


def local(query, key, value, gain, cotangent, query2, key2, softmax_values):
    tokens, heads, width = query.shape
    flat = (tokens * heads, width)
    head_major = (heads, tokens, width)
    square = (heads, width, width)
    unit = 2 * tokens * tokens * width * heads
    ring = lax.axis_size(CTX)
    members = lax.axis_size(HEADS)
    token_buffer = pltpu.VMEM(query.shape, bf16)
    flat_buffer = pltpu.VMEM(flat, f32)

    def sems(n):
        return pltpu.SemaphoreType.DMA((n,))

    def onward(x):
        return lax.ppermute(x, CTX, [(i, i + 1) for i in range(ring - 1)])

    have = jnp.minimum(lax.axis_index(CTX), WINDOW_BLOCKS - 1).astype(jnp.int32).reshape(1)
    key, value, have = tied(key, value, have)

    (kh,) = call(head_major_kernel, [shape(head_major, bf16)], [key], [flat_buffer])
    vh, states = call(
        state_kernel,
        [shape(head_major, bf16), shape(square, bf16)],
        [kh, value],
        [flat_buffer],
        unit // 4,
    )
    states, query, cotangent = tied(states, query, cotangent)
    pieces, kh, vh = tied(spread(states), kh, vh)
    total, kv0 = call(
        total_kernel,
        [shape(square[1:], bf16), shape((2, tokens, width), bf16)],
        [pieces, key2[:, 0], softmax_values[:, 0]],
    )
    total, kh, vh = tied(total, kh, vh)
    kv1 = onward(kv0)
    totals = [from_row(total, d, False) for d in (1, 3, 2)]
    qh, gh, loc = call(
        local_kernel,
        [shape(head_major, bf16), shape(head_major, f32), shape(head_major, f32)],
        [query, cotangent, gain, kh, vh],
        [flat_buffer, flat_buffer],
        2 * unit,
    )
    *totals, kv1, loc = tied(*totals, kv1, loc)
    prefix, kv1 = tied(spread(scanned(pieces, totals, False)), kv1)
    kv2 = onward(kv1)
    att, part = call(
        attention_kernel,
        [shape(head_major, f32), shape((members, 2, tokens), f32)],
        [loc, qh, gh, prefix],
        (),
        unit // 4,
    )
    gathered = lax.all_to_all(part, HEADS, 0, 0, tiled=True)
    gathered, kv2 = tied(gathered, kv2)
    da, block_grad, inverse = call(
        backward_kernel,
        [shape(head_major, bf16), shape(square, bf16), shape((tokens, width), f32)],
        [gathered, att, gh, qh],
        (),
        unit // 4,
    )
    back_pieces, att, da, inverse, kv2 = tied(spread(block_grad), att, da, inverse, kv2)
    kv3 = onward(kv2)
    back_total = row_total(back_pieces)
    back_near = from_row(back_total, 1, True)
    gq, normed, sq = call(
        query_gradient_kernel,
        [shape(query.shape, bf16), shape(query.shape, bf16), shape(flat, bf16)],
        [kh, vh, da, prefix, att, inverse, gain, query2],
        [flat_buffer, flat_buffer],
        2 * unit,
    )
    back_near, gq, da = tied(back_near, gq, da)
    back_far = from_row(pair_total(back_total, back_near), 2, True)
    pk, pv = call(
        key_value_local_kernel, [shape(head_major, bf16)] * 2, [qh, kh, vh, da], (), 4 * unit
    )
    back_far, pk, sq, kv3 = tied(back_far, pk, sq, kv3)
    suffix, sq = tied(spread(scanned(back_pieces, [back_near, back_far], True)), sq)
    normed, gq, gk, gv, attended = call(
        final_kernel,
        [shape(query.shape, bf16)] * 5,
        [have, sq, kv0, kv1, kv2, kv3, kh, vh, pk, pv, suffix, gq, normed],
        [
            token_buffer,
            pltpu.VMEM((2, WINDOW_BLOCKS, tokens, tokens), f32),
            flat_buffer,
            flat_buffer,
            token_buffer,
            token_buffer,
            sems(4),
            sems(2),
            pltpu.SemaphoreType.DMA((4, 2)),
        ],
        9 * unit,
        smem_first=True,
        vmem=32,
        hbm_out=range(5),
    )
    return normed, gq, gk, gv, attended


def solution(mesh):
    sizes = (4, 8, 4, 2)
    fine = Mesh(mesh.devices.reshape(sizes), ("y", "z", "x", "core"))
    tokens = P(CTX, HEADS, None)
    return jax.shard_map(
        local,
        mesh=fine,
        in_specs=(tokens, tokens, tokens, P(HEADS, None), tokens, tokens, tokens, tokens),
        out_specs=(tokens,) * 5,
        check_vma=False,
    )
```

```python
import functools
import jax
import jax.numpy as jnp
from jax import lax
from jax.experimental import pallas as pl
from jax.experimental.pallas import tpu as pltpu
from jax.sharding import Mesh, PartitionSpec as P

ATTN_HEADS = 64
HEAD_WIDTH = 128
WINDOW_BLOCKS = 4
CHANNELS = ATTN_HEADS * HEAD_WIDTH
EPSILON = 1e-06
LOG2E = 1.4426950408889634

f32 = jnp.float32
bf16 = jnp.bfloat16
MIB = 1 << 20
HEADS = ("x", "core")
CTX = ("y", "z")


def nn(a, b, precision=None):
    return lax.dot_general(
        a, b, (((1,), (0,)), ((), ())), precision=precision, preferred_element_type=f32
    )


def nt(a, b, precision=None):
    return lax.dot_general(
        a, b, (((1,), (1,)), ((), ())), precision=precision, preferred_element_type=f32
    )


def tn(a, b, precision=None):
    return lax.dot_general(
        a, b, (((0,), (0,)), ((), ())), precision=precision, preferred_element_type=f32
    )


def call(kernel, out_shapes, args, scratch=(), flops=0, smem_first=False, vmem=20, hbm_in=(), hbm_out=()):
    def place(i, far):
        return pl.BlockSpec(memory_space=pltpu.HBM if i in far else pltpu.VMEM)

    specs = [place(i, hbm_in) for i in range(len(args))]
    if smem_first:
        specs[0] = pl.BlockSpec(memory_space=pltpu.SMEM)
    moved = sum(a.size * a.dtype.itemsize for a in (*args, *out_shapes))
    return pl.pallas_call(
        kernel,
        out_shape=out_shapes,
        in_specs=specs,
        out_specs=[place(i, hbm_out) for i in range(len(out_shapes))],
        scratch_shapes=list(scratch),
        compiler_params=pltpu.CompilerParams(vmem_limit_bytes=vmem * MIB),
        cost_estimate=pl.CostEstimate(flops=flops, bytes_accessed=moved, transcendentals=0),
    )(*args)


def shape(dims, dtype):
    return jax.ShapeDtypeStruct(dims, dtype)


def fetch(pairs, sems):
    copies = []
    for i, (src, dst) in enumerate(pairs):
        copy = pltpu.make_async_copy(src, dst, sems.at[i])
        copy.start()
        copies.append(copy)
    return copies


def head_major_kernel(x_ref, out_ref, flat):
    tokens, heads, width = x_ref.shape
    flat[...] = x_ref[...].astype(f32).reshape(tokens * heads, width)
    for h in range(heads):
        out_ref[h] = flat[pl.ds(h, tokens, stride=heads), :].astype(bf16)


def state_kernel(kh_ref, v_ref, vh_ref, st_ref, vs):
    tokens, heads, width = v_ref.shape
    vs[...] = v_ref[...].astype(f32).reshape(tokens * heads, width)
    for h in range(heads):
        vh = vs[pl.ds(h, tokens, stride=heads), :].astype(bf16)
        vh_ref[h] = vh
        st_ref[h] = tn(kh_ref[h], vh).astype(bf16)


def each(count, body, unroll=8):
    def step(i, carry):
        body(i)
        return carry

    lax.fori_loop(0, count, step, 0, unroll=unroll)


def causal_below(rows):
    r = lax.broadcasted_iota(jnp.int32, (rows, rows), 0)
    c = lax.broadcasted_iota(jnp.int32, (rows, rows), 1)
    return c <= r


def local_kernel(q_ref, c_ref, gain_ref, kh_ref, vh_ref, qh_ref, gh_ref, loc_ref, qs, cs):
    tokens, heads, width = q_ref.shape
    half = tokens // 2
    qs[...] = q_ref[...].astype(f32).reshape(tokens * heads, width)
    cs[...] = (c_ref[...].astype(f32) * gain_ref[...][None]).reshape(tokens * heads, width)
    causal = causal_below(half)

    def head(h):
        qh = qs[pl.ds(h, tokens, stride=heads), :].astype(bf16)
        qh_ref[h] = qh
        gh_ref[h] = cs[pl.ds(h, tokens, stride=heads), :]
        kh = kh_ref[h]
        vh = vh_ref[h]
        w0 = jnp.where(causal, nt(qh[:half], kh[:half]), 0.0).astype(bf16)
        w10 = nt(qh[half:], kh[:half]).astype(bf16)
        w11 = jnp.where(causal, nt(qh[half:], kh[half:]), 0.0).astype(bf16)
        loc_ref[h, :half] = nn(w0, vh[:half])
        loc_ref[h, half:] = nn(w10, vh[:half]) + nn(w11, vh[half:])

    each(heads, head)


def terms(x):
    parts = []
    for _ in range(3):
        high = x.astype(bf16)
        parts.append(high)
        x = x - high.astype(f32)
    return parts


def attention_kernel(loc_ref, qh_ref, gh_ref, pre_ref, att_ref, part_ref):
    heads, tokens, width = loc_ref.shape
    squares = jnp.zeros((tokens, width), f32)
    inner = jnp.zeros((tokens, width), f32)
    for h in range(heads):
        att = loc_ref[h] + nn(qh_ref[h], pre_ref[h])
        att_ref[h] = att
        squares = squares + att * att
        inner = inner + att * gh_ref[h]
    ones = jnp.ones((8, width), bf16)
    rows = jnp.concatenate(
        [sum(nt(ones, part) for part in terms(x))[0:1] for x in (squares, inner)]
    )
    for j in range(part_ref.shape[0]):
        part_ref[j] = rows


def row_scales(g_ref):
    ones = jnp.ones((g_ref.shape[0], HEAD_WIDTH), bf16)
    squares = sum(tn(part, ones) for part in terms(g_ref[:, 0, :]))
    inner = sum(tn(part, ones) for part in terms(g_ref[:, 1, :]))
    inverse = 1.0 / jnp.sqrt(squares / CHANNELS + EPSILON)
    return inverse, inverse * inner / CHANNELS


def backward_kernel(g_ref, att_ref, gh_ref, qh_ref, da_ref, bg_ref, inv_ref):
    inverse, mean = row_scales(g_ref)
    inv_ref[...] = inverse
    scaled = inverse * mean
    for h in range(att_ref.shape[0]):
        d = ((gh_ref[h] - att_ref[h] * scaled) * inverse).astype(bf16)
        da_ref[h] = d
        bg_ref[h] = tn(qh_ref[h], d).astype(bf16)


def final_kernel(
    pos_ref, sq_ref, kv0, kv1, kv2, kv3,
    kh_ref, vh_ref, pk_ref, pv_ref, suf_ref, gq_ref, norm_ref,
    norm_hbm, gq_hbm, gk_hbm, gv_hbm, out_hbm,
    out, ahead, ks, vs, kb, vb, sems, done_sems, grad_sems,
):
    tokens, heads, width = out.shape
    kv = (kv0, kv1, kv2, kv3)
    copies = fetch([(norm_ref, norm_hbm), (gq_ref, gq_hbm)], done_sems)
    pieces = grad_sems.shape[0]
    rows = tokens // pieces

    def grad_copies(i):
        part = pl.ds(i * rows, rows)
        pairs = ((kb, gk_hbm), (vb, gv_hbm))
        return [
            pltpu.make_async_copy(b.at[part], target.at[part], grad_sems.at[i, j])
            for j, (b, target) in enumerate(pairs)
        ]

    def finish():
        for i in range(pieces):
            part, flat = pl.ds(i * rows, rows), pl.ds(i * rows * heads, rows * heads)
            for h in range(heads):
                suf = suf_ref[h]
                target = pl.ds(i * rows * heads + h, rows, stride=heads)
                ks[target, :] = pk_ref[h, part].astype(f32) + nt(vh_ref[h, part], suf)
                vs[target, :] = pv_ref[h, part].astype(f32) + nn(kh_ref[h, part], suf)
            for src, buffer in ((ks, kb), (vs, vb)):
                buffer[part] = src[flat, :].astype(bf16).reshape(rows, heads, width)
            for copy in grad_copies(i):
                copy.start()

    scale = LOG2E * HEAD_WIDTH ** (-0.5)
    ones = jnp.ones((tokens, width), bf16)
    quarters = 4
    quarter = tokens // quarters

    def scores(chunk, rows, count):
        q = sq_ref[pl.ds(pl.multiple_of(chunk * rows, rows), rows), :]
        row = chunk * rows + lax.broadcasted_iota(jnp.int32, (rows, tokens), 0)
        column = lax.broadcasted_iota(jnp.int32, (rows, tokens), 1)
        own = jnp.where(column <= row // heads, nt(q, kv[0][0]), -1e30)
        return [own] + [nt(q, kv[b][0]) for b in range(1, count)]

    def weigh(parts, chunk, rows):
        top = None
        for s in parts:
            for j in range(0, tokens, 128):
                piece = s[:, j : j + 128]
                top = piece if top is None else jnp.maximum(top, piece)
        top = jnp.max(top, axis=1, keepdims=True) * scale
        total = None
        for b, s in enumerate(parts):
            p = jnp.exp2(s * scale - top).astype(bf16)
            o = nn(p, jnp.concatenate([kv[b][1], ones], axis=1))
            total = o if total is None else total + o
        chunk_tokens = rows // heads
        t0 = pl.multiple_of(chunk * chunk_tokens, chunk_tokens)
        out[pl.ds(t0, chunk_tokens)] = (
            (total[:, :width] / total[:, width:]).astype(bf16).reshape(chunk_tokens, heads, width)
        )

    def store(i):
        part = pl.ds(pl.multiple_of(i * quarter, quarter), quarter)
        return pltpu.make_async_copy(out.at[part], out_hbm.at[part], sems.at[i])

    def run(count):
        finish()
        rows = 256
        per = quarter * heads // rows

        def body(i, carry):
            for j in range(per):
                chunk = i * per + j
                weigh(scores(chunk, rows, count), chunk, rows)
            store(i).start()
            return carry

        lax.fori_loop(0, quarters, body, 0)

    def run_ahead():
        rows = 512
        per = quarter * heads // rows
        last = quarters * per - 1

        def put(slot, chunk):
            for b, s in enumerate(scores(chunk, rows, WINDOW_BLOCKS)):
                ahead[slot, b] = s

        def body(i, carry):
            for j in range(per):
                chunk = i * per + j
                put((j + 1) % 2, jnp.minimum(chunk + 1, last))
                weigh([ahead[j % 2, b] for b in range(WINDOW_BLOCKS)], chunk, rows)
            store(i).start()
            return carry

        put(0, 0)
        finish()
        lax.fori_loop(0, quarters, body, 0)

    have = pos_ref[0]
    for count in range(1, WINDOW_BLOCKS):
        pl.when(have == count - 1)(functools.partial(run, count))
    pl.when(have == WINDOW_BLOCKS - 1)(run_ahead)
    for i in range(quarters):
        store(i).wait()
    for i in range(pieces):
        copies += grad_copies(i)
    for copy in copies:
        copy.wait()


def query_gradient_kernel(
    kh_ref, vh_ref, da_ref, pre_ref, att_ref, inv_ref, gain_ref, q2_ref,
    gq_ref, norm_ref, sq_ref, qs, ns,
):
    heads, tokens, width = kh_ref.shape
    half = tokens // 2
    below = causal_below(half)
    lo, hi = slice(0, half), slice(half, tokens)
    inverse = inv_ref[...]
    for h in range(heads):
        k, v, da = kh_ref[h], vh_ref[h], da_ref[h]
        d00 = jnp.where(below, nt(da[lo], v[lo]), 0.0).astype(bf16)
        d10 = nt(da[hi], v[lo]).astype(bf16)
        d11 = jnp.where(below, nt(da[hi], v[hi]), 0.0).astype(bf16)
        gq = nt(da, pre_ref[h])
        ns[pl.ds(h, tokens, stride=heads), :] = gain_ref[h : h + 1, :] * (att_ref[h] * inverse)
        qs[pl.ds(h, half, stride=heads), :] = gq[lo] + nn(d00, k[lo])
        qs[pl.ds(half * heads + h, half, stride=heads), :] = (
            gq[hi] + nn(d10, k[lo]) + nn(d11, k[hi])
        )
    gq_ref[...] = qs[...].astype(bf16).reshape(tokens, heads, width)
    n = ns[...].astype(bf16)
    norm_ref[...] = n.reshape(tokens, heads, width)
    q2 = q2_ref[...].astype(f32).reshape(tokens * heads, width)
    sq_ref[...] = (q2 + n.astype(f32)).astype(bf16)


def key_value_local_kernel(qh_ref, kh_ref, vh_ref, da_ref, gk_ref, gv_ref):
    heads, tokens, width = qh_ref.shape
    half = tokens // 2
    r = lax.broadcasted_iota(jnp.int32, (half, half), 0)
    c = lax.broadcasted_iota(jnp.int32, (half, half), 1)
    above = r <= c
    lo, hi = slice(0, half), slice(half, tokens)

    def up(x):
        return jnp.where(above, x, 0.0).astype(bf16)

    def head(h):
        q, k, v, da = qh_ref[h], kh_ref[h], vh_ref[h], da_ref[h]
        for out, a, b, other in ((gk_ref, v, da, q), (gv_ref, k, q, da)):
            m00 = up(nt(a[lo], b[lo]))
            m01 = nt(a[lo], b[hi]).astype(bf16)
            m11 = up(nt(a[hi], b[hi]))
            out[h, :half] = (nn(m00, other[lo]) + nn(m01, other[hi])).astype(bf16)
            out[h, half:] = nn(m11, other[hi]).astype(bf16)

    each(heads, head)


def scan_kernel(back, recv_ref, *refs):
    *others, out_ref = refs
    count = recv_ref.shape[0]
    running = sum(other[...].astype(f32) for other in others)
    order = range(count) if back else range(count - 1, -1, -1)
    for i in order:
        out_ref[i] = running.astype(bf16)
        running = running + recv_ref[i].astype(f32)


def pair_kernel(own_ref, other_ref, out_ref):
    out_ref[...] = (own_ref[...].astype(f32) + other_ref[...].astype(f32)).astype(bf16)


def total_kernel(recv_ref, *refs):
    *sources, out_ref = refs[:3]
    for j, source in enumerate(sources):
        refs[3][j] = source[...]
    total = recv_ref[0].astype(f32)
    for i in range(1, recv_ref.shape[0]):
        total = total + recv_ref[i].astype(f32)
    out_ref[...] = total.astype(bf16)


def tied(*values):
    return lax.optimization_barrier(values)


def row_total(pieces):
    return call(total_kernel, [shape(pieces.shape[1:], bf16)], [pieces])[0]


def from_row(x, d, back):
    rows = lax.axis_size("y")
    return lax.ppermute(x, "y", [(i + d, i) if back else (i, i + d) for i in range(rows - d)])


def pair_total(own, other):
    return call(pair_kernel, [shape(own.shape, bf16)], [own, other])[0]


def scanned(pieces, totals, back):
    return call(
        functools.partial(scan_kernel, back), [shape(pieces.shape, bf16)], [pieces, *totals]
    )[0]


def spread(x):
    members = list(range(lax.axis_size("z")))[::-1]
    return lax.all_to_all(x, "z", 0, 0, tiled=True, axis_index_groups=[members])


def local(query, key, value, gain, cotangent, query2, key2, softmax_values):
    tokens, heads, width = query.shape
    flat = (tokens * heads, width)
    head_major = (heads, tokens, width)
    square = (heads, width, width)
    unit = 2 * tokens * tokens * width * heads
    ring = lax.axis_size(CTX)
    members = lax.axis_size(HEADS)
    token_buffer = pltpu.VMEM(query.shape, bf16)
    flat_buffer = pltpu.VMEM(flat, f32)

    def sems(n):
        return pltpu.SemaphoreType.DMA((n,))

    def onward(x):
        return lax.ppermute(x, CTX, [(i, i + 1) for i in range(ring - 1)])

    have = jnp.minimum(lax.axis_index(CTX), WINDOW_BLOCKS - 1).astype(jnp.int32).reshape(1)
    key, value, have = tied(key, value, have)

    (kh,) = call(head_major_kernel, [shape(head_major, bf16)], [key], [flat_buffer])
    vh, states = call(
        state_kernel,
        [shape(head_major, bf16), shape(square, bf16)],
        [kh, value],
        [flat_buffer],
        unit // 4,
    )
    states, query, cotangent = tied(states, query, cotangent)
    pieces, kh, vh = tied(spread(states), kh, vh)
    total, kv0 = call(
        total_kernel,
        [shape(square[1:], bf16), shape((2, tokens, width), bf16)],
        [pieces, key2[:, 0], softmax_values[:, 0]],
    )
    total, kh, vh = tied(total, kh, vh)
    kv1 = onward(kv0)
    totals = [from_row(total, d, False) for d in (1, 3, 2)]
    qh, gh, loc = call(
        local_kernel,
        [shape(head_major, bf16), shape(head_major, f32), shape(head_major, f32)],
        [query, cotangent, gain, kh, vh],
        [flat_buffer, flat_buffer],
        2 * unit,
    )
    *totals, kv1, loc = tied(*totals, kv1, loc)
    prefix, kv1 = tied(spread(scanned(pieces, totals, False)), kv1)
    kv2 = onward(kv1)
    att, part = call(
        attention_kernel,
        [shape(head_major, f32), shape((members, 2, tokens), f32)],
        [loc, qh, gh, prefix],
        (),
        unit // 4,
    )
    gathered = lax.all_to_all(part, HEADS, 0, 0, tiled=True)
    gathered, kv2 = tied(gathered, kv2)
    da, block_grad, inverse = call(
        backward_kernel,
        [shape(head_major, bf16), shape(square, bf16), shape((tokens, width), f32)],
        [gathered, att, gh, qh],
        (),
        unit // 4,
    )
    back_pieces, att, da, inverse, kv2 = tied(spread(block_grad), att, da, inverse, kv2)
    kv3 = onward(kv2)
    back_total = row_total(back_pieces)
    back_near = from_row(back_total, 1, True)
    gq, normed, sq = call(
        query_gradient_kernel,
        [shape(query.shape, bf16), shape(query.shape, bf16), shape(flat, bf16)],
        [kh, vh, da, prefix, att, inverse, gain, query2],
        [flat_buffer, flat_buffer],
        2 * unit,
    )
    back_near, gq, da = tied(back_near, gq, da)
    back_far = from_row(pair_total(back_total, back_near), 2, True)
    pk, pv = call(
        key_value_local_kernel, [shape(head_major, bf16)] * 2, [qh, kh, vh, da], (), 4 * unit
    )
    back_far, pk, sq, kv3 = tied(back_far, pk, sq, kv3)
    suffix, sq = tied(spread(scanned(back_pieces, [back_near, back_far], True)), sq)
    normed, gq, gk, gv, attended = call(
        final_kernel,
        [shape(query.shape, bf16)] * 5,
        [have, sq, kv0, kv1, kv2, kv3, kh, vh, pk, pv, suffix, gq, normed],
        [
            token_buffer,
            pltpu.VMEM((2, WINDOW_BLOCKS, tokens, tokens), f32),
            flat_buffer,
            flat_buffer,
            token_buffer,
            token_buffer,
            sems(4),
            sems(2),
            pltpu.SemaphoreType.DMA((4, 2)),
        ],
        9 * unit,
        smem_first=True,
        vmem=32,
        hbm_out=range(5),
    )
    return normed, gq, gk, gv, attended


def solution(mesh):
    sizes = (4, 8, 4, 2)
    fine = Mesh(mesh.devices.reshape(sizes), ("y", "z", "x", "core"))
    tokens = P(CTX, HEADS, None)
    return jax.shard_map(
        local,
        mesh=fine,
        in_specs=(tokens, tokens, tokens, P(HEADS, None), tokens, tokens, tokens, tokens),
        out_specs=(tokens,) * 5,
        check_vma=False,
    )
```

```python
import functools
import jax
import jax.numpy as jnp
from jax import lax
from jax.experimental import pallas as pl
from jax.experimental.pallas import tpu as pltpu
from jax.sharding import Mesh, PartitionSpec as P

ATTN_HEADS = 64
HEAD_WIDTH = 128
WINDOW_BLOCKS = 4
CHANNELS = ATTN_HEADS * HEAD_WIDTH
EPSILON = 1e-06
LOG2E = 1.4426950408889634

f32 = jnp.float32
bf16 = jnp.bfloat16
MIB = 1 << 20
HEADS = ("x", "core")
CTX = ("y", "z")


def nn(a, b, precision=None):
    return lax.dot_general(
        a, b, (((1,), (0,)), ((), ())), precision=precision, preferred_element_type=f32
    )


def nt(a, b, precision=None):
    return lax.dot_general(
        a, b, (((1,), (1,)), ((), ())), precision=precision, preferred_element_type=f32
    )


def tn(a, b, precision=None):
    return lax.dot_general(
        a, b, (((0,), (0,)), ((), ())), precision=precision, preferred_element_type=f32
    )


def call(kernel, out_shapes, args, scratch=(), flops=0, smem_first=False, vmem=20, hbm_in=(), hbm_out=()):
    def place(i, far):
        return pl.BlockSpec(memory_space=pltpu.HBM if i in far else pltpu.VMEM)

    specs = [place(i, hbm_in) for i in range(len(args))]
    if smem_first:
        specs[0] = pl.BlockSpec(memory_space=pltpu.SMEM)
    moved = sum(a.size * a.dtype.itemsize for a in (*args, *out_shapes))
    return pl.pallas_call(
        kernel,
        out_shape=out_shapes,
        in_specs=specs,
        out_specs=[place(i, hbm_out) for i in range(len(out_shapes))],
        scratch_shapes=list(scratch),
        compiler_params=pltpu.CompilerParams(vmem_limit_bytes=vmem * MIB),
        cost_estimate=pl.CostEstimate(flops=flops, bytes_accessed=moved, transcendentals=0),
    )(*args)


def shape(dims, dtype):
    return jax.ShapeDtypeStruct(dims, dtype)


def fetch(pairs, sems):
    copies = []
    for i, (src, dst) in enumerate(pairs):
        copy = pltpu.make_async_copy(src, dst, sems.at[i])
        copy.start()
        copies.append(copy)
    return copies


def head_major_kernel(x_ref, out_ref, flat):
    tokens, heads, width = x_ref.shape
    flat[...] = x_ref[...].astype(f32).reshape(tokens * heads, width)
    for h in range(heads):
        out_ref[h] = flat[pl.ds(h, tokens, stride=heads), :].astype(bf16)


def state_kernel(kh_ref, v_ref, vh_ref, st_ref, vs):
    tokens, heads, width = v_ref.shape
    vs[...] = v_ref[...].astype(f32).reshape(tokens * heads, width)
    for h in range(heads):
        vh = vs[pl.ds(h, tokens, stride=heads), :].astype(bf16)
        vh_ref[h] = vh
        st_ref[h] = tn(kh_ref[h], vh).astype(bf16)


def each(count, body, unroll=8):
    def step(i, carry):
        body(i)
        return carry

    lax.fori_loop(0, count, step, 0, unroll=unroll)


def causal_below(rows):
    r = lax.broadcasted_iota(jnp.int32, (rows, rows), 0)
    c = lax.broadcasted_iota(jnp.int32, (rows, rows), 1)
    return c <= r


def local_kernel(q_ref, c_ref, gain_ref, kh_ref, vh_ref, qh_ref, gh_ref, loc_ref, qs, cs):
    tokens, heads, width = q_ref.shape
    half = tokens // 2
    qs[...] = q_ref[...].astype(f32).reshape(tokens * heads, width)
    cs[...] = (c_ref[...].astype(f32) * gain_ref[...][None]).reshape(tokens * heads, width)
    causal = causal_below(half)

    def head(h):
        qh = qs[pl.ds(h, tokens, stride=heads), :].astype(bf16)
        qh_ref[h] = qh
        gh_ref[h] = cs[pl.ds(h, tokens, stride=heads), :]
        kh = kh_ref[h]
        vh = vh_ref[h]
        w0 = jnp.where(causal, nt(qh[:half], kh[:half]), 0.0).astype(bf16)
        w10 = nt(qh[half:], kh[:half]).astype(bf16)
        w11 = jnp.where(causal, nt(qh[half:], kh[half:]), 0.0).astype(bf16)
        loc_ref[h, :half] = nn(w0, vh[:half])
        loc_ref[h, half:] = nn(w10, vh[:half]) + nn(w11, vh[half:])

    each(heads, head)


def terms(x):
    parts = []
    for _ in range(3):
        high = x.astype(bf16)
        parts.append(high)
        x = x - high.astype(f32)
    return parts


def attention_kernel(loc_ref, qh_ref, gh_ref, pre_ref, att_ref, part_ref):
    heads, tokens, width = loc_ref.shape
    squares = jnp.zeros((tokens, width), f32)
    inner = jnp.zeros((tokens, width), f32)
    for h in range(heads):
        att = loc_ref[h] + nn(qh_ref[h], pre_ref[h])
        att_ref[h] = att
        squares = squares + att * att
        inner = inner + att * gh_ref[h]
    ones = jnp.ones((8, width), bf16)
    rows = jnp.concatenate(
        [sum(nt(ones, part) for part in terms(x))[0:1] for x in (squares, inner)]
    )
    for j in range(part_ref.shape[0]):
        part_ref[j] = rows


def row_scales(g_ref):
    ones = jnp.ones((g_ref.shape[0], HEAD_WIDTH), bf16)
    squares = sum(tn(part, ones) for part in terms(g_ref[:, 0, :]))
    inner = sum(tn(part, ones) for part in terms(g_ref[:, 1, :]))
    inverse = 1.0 / jnp.sqrt(squares / CHANNELS + EPSILON)
    return inverse, inverse * inner / CHANNELS


def backward_kernel(g_ref, att_ref, gh_ref, qh_ref, da_ref, bg_ref, inv_ref):
    inverse, mean = row_scales(g_ref)
    inv_ref[...] = inverse
    scaled = inverse * mean
    for h in range(att_ref.shape[0]):
        d = ((gh_ref[h] - att_ref[h] * scaled) * inverse).astype(bf16)
        da_ref[h] = d
        bg_ref[h] = tn(qh_ref[h], d).astype(bf16)


def final_kernel(
    pos_ref, sq_ref, kv0, kv1, kv2, kv3,
    kh_ref, vh_ref, pk_ref, pv_ref, suf_ref, gq_ref, norm_ref,
    norm_hbm, gq_hbm, gk_hbm, gv_hbm, out_hbm,
    out, ahead, ks, vs, kb, vb, sems, done_sems, grad_sems,
):
    tokens, heads, width = out.shape
    kv = (kv0, kv1, kv2, kv3)
    copies = fetch([(norm_ref, norm_hbm), (gq_ref, gq_hbm)], done_sems)
    pieces = grad_sems.shape[0]
    rows = tokens // pieces

    def grad_copies(i):
        part = pl.ds(i * rows, rows)
        pairs = ((kb, gk_hbm), (vb, gv_hbm))
        return [
            pltpu.make_async_copy(b.at[part], target.at[part], grad_sems.at[i, j])
            for j, (b, target) in enumerate(pairs)
        ]

    def finish():
        for i in range(pieces):
            part, flat = pl.ds(i * rows, rows), pl.ds(i * rows * heads, rows * heads)
            for h in range(heads):
                suf = suf_ref[h]
                target = pl.ds(i * rows * heads + h, rows, stride=heads)
                ks[target, :] = pk_ref[h, part].astype(f32) + nt(vh_ref[h, part], suf)
                vs[target, :] = pv_ref[h, part].astype(f32) + nn(kh_ref[h, part], suf)
            for src, buffer in ((ks, kb), (vs, vb)):
                buffer[part] = src[flat, :].astype(bf16).reshape(rows, heads, width)
            for copy in grad_copies(i):
                copy.start()

    scale = LOG2E * HEAD_WIDTH ** (-0.5)
    ones = jnp.ones((tokens, width), bf16)
    quarters = 8
    quarter = tokens // quarters

    def scores(chunk, rows, count):
        q = sq_ref[pl.ds(pl.multiple_of(chunk * rows, rows), rows), :]
        row = chunk * rows + lax.broadcasted_iota(jnp.int32, (rows, tokens), 0)
        column = lax.broadcasted_iota(jnp.int32, (rows, tokens), 1)
        own = jnp.where(column <= row // heads, nt(q, kv[0][0]), -1e30)
        return [own] + [nt(q, kv[b][0]) for b in range(1, count)]

    def weigh(parts, chunk, rows):
        top = None
        for s in parts:
            for j in range(0, tokens, 128):
                piece = s[:, j : j + 128]
                top = piece if top is None else jnp.maximum(top, piece)
        top = jnp.max(top, axis=1, keepdims=True) * scale
        total = None
        for b, s in enumerate(parts):
            p = jnp.exp2(s * scale - top).astype(bf16)
            o = nn(p, jnp.concatenate([kv[b][1], ones], axis=1))
            total = o if total is None else total + o
        chunk_tokens = rows // heads
        t0 = pl.multiple_of(chunk * chunk_tokens, chunk_tokens)
        out[pl.ds(t0, chunk_tokens)] = (
            (total[:, :width] / total[:, width:]).astype(bf16).reshape(chunk_tokens, heads, width)
        )

    def store(i):
        part = pl.ds(pl.multiple_of(i * quarter, quarter), quarter)
        return pltpu.make_async_copy(out.at[part], out_hbm.at[part], sems.at[i])

    def run(count):
        finish()
        rows = 256
        per = quarter * heads // rows

        def body(i, carry):
            for j in range(per):
                chunk = i * per + j
                weigh(scores(chunk, rows, count), chunk, rows)
            store(i).start()
            return carry

        lax.fori_loop(0, quarters, body, 0)

    def run_ahead():
        rows = quarter * heads
        per = 2
        last = quarters - 1

        def put(slot, chunk):
            for b, s in enumerate(scores(chunk, rows, WINDOW_BLOCKS)):
                ahead[slot, b] = s

        def body(i, carry):
            for j in range(per):
                chunk = i * per + j
                put((j + 1) % 2, jnp.minimum(chunk + 1, last))
                weigh([ahead[j % 2, b] for b in range(WINDOW_BLOCKS)], chunk, rows)
                store(chunk).start()
            return carry

        put(0, 0)
        finish()
        lax.fori_loop(0, quarters // per, body, 0)

    have = pos_ref[0]
    for count in range(1, WINDOW_BLOCKS):
        pl.when(have == count - 1)(functools.partial(run, count))
    pl.when(have == WINDOW_BLOCKS - 1)(run_ahead)
    for i in range(quarters):
        store(i).wait()
    for i in range(pieces):
        copies += grad_copies(i)
    for copy in copies:
        copy.wait()


def query_gradient_kernel(
    kh_ref, vh_ref, da_ref, pre_ref, att_ref, inv_ref, gain_ref, q2_ref,
    gq_ref, norm_ref, sq_ref, qs, ns,
):
    heads, tokens, width = kh_ref.shape
    half = tokens // 2
    below = causal_below(half)
    lo, hi = slice(0, half), slice(half, tokens)
    inverse = inv_ref[...]
    for h in range(heads):
        k, v, da = kh_ref[h], vh_ref[h], da_ref[h]
        d00 = jnp.where(below, nt(da[lo], v[lo]), 0.0).astype(bf16)
        d10 = nt(da[hi], v[lo]).astype(bf16)
        d11 = jnp.where(below, nt(da[hi], v[hi]), 0.0).astype(bf16)
        gq = nt(da, pre_ref[h])
        ns[pl.ds(h, tokens, stride=heads), :] = gain_ref[h : h + 1, :] * (att_ref[h] * inverse)
        qs[pl.ds(h, half, stride=heads), :] = gq[lo] + nn(d00, k[lo])
        qs[pl.ds(half * heads + h, half, stride=heads), :] = (
            gq[hi] + nn(d10, k[lo]) + nn(d11, k[hi])
        )
    gq_ref[...] = qs[...].astype(bf16).reshape(tokens, heads, width)
    n = ns[...].astype(bf16)
    norm_ref[...] = n.reshape(tokens, heads, width)
    q2 = q2_ref[...].astype(f32).reshape(tokens * heads, width)
    sq_ref[...] = (q2 + n.astype(f32)).astype(bf16)


def key_value_local_kernel(qh_ref, kh_ref, vh_ref, da_ref, gk_ref, gv_ref):
    heads, tokens, width = qh_ref.shape
    half = tokens // 2
    r = lax.broadcasted_iota(jnp.int32, (half, half), 0)
    c = lax.broadcasted_iota(jnp.int32, (half, half), 1)
    above = r <= c
    lo, hi = slice(0, half), slice(half, tokens)

    def up(x):
        return jnp.where(above, x, 0.0).astype(bf16)

    def head(h):
        q, k, v, da = qh_ref[h], kh_ref[h], vh_ref[h], da_ref[h]
        for out, a, b, other in ((gk_ref, v, da, q), (gv_ref, k, q, da)):
            m00 = up(nt(a[lo], b[lo]))
            m01 = nt(a[lo], b[hi]).astype(bf16)
            m11 = up(nt(a[hi], b[hi]))
            out[h, :half] = (nn(m00, other[lo]) + nn(m01, other[hi])).astype(bf16)
            out[h, half:] = nn(m11, other[hi]).astype(bf16)

    each(heads, head)


def scan_kernel(back, recv_ref, *refs):
    *others, out_ref = refs
    count = recv_ref.shape[0]
    running = sum(other[...].astype(f32) for other in others)
    order = range(count) if back else range(count - 1, -1, -1)
    for i in order:
        out_ref[i] = running.astype(bf16)
        running = running + recv_ref[i].astype(f32)


def pair_kernel(own_ref, other_ref, out_ref):
    out_ref[...] = (own_ref[...].astype(f32) + other_ref[...].astype(f32)).astype(bf16)


def total_kernel(recv_ref, *refs):
    *sources, out_ref = refs[:3]
    for j, source in enumerate(sources):
        refs[3][j] = source[...]
    total = recv_ref[0].astype(f32)
    for i in range(1, recv_ref.shape[0]):
        total = total + recv_ref[i].astype(f32)
    out_ref[...] = total.astype(bf16)


def tied(*values):
    return lax.optimization_barrier(values)


def row_total(pieces):
    return call(total_kernel, [shape(pieces.shape[1:], bf16)], [pieces])[0]


def from_row(x, d, back):
    rows = lax.axis_size("y")
    return lax.ppermute(x, "y", [(i + d, i) if back else (i, i + d) for i in range(rows - d)])


def pair_total(own, other):
    return call(pair_kernel, [shape(own.shape, bf16)], [own, other])[0]


def scanned(pieces, totals, back):
    return call(
        functools.partial(scan_kernel, back), [shape(pieces.shape, bf16)], [pieces, *totals]
    )[0]


def spread(x):
    members = list(range(lax.axis_size("z")))[::-1]
    return lax.all_to_all(x, "z", 0, 0, tiled=True, axis_index_groups=[members])


def local(query, key, value, gain, cotangent, query2, key2, softmax_values):
    tokens, heads, width = query.shape
    flat = (tokens * heads, width)
    head_major = (heads, tokens, width)
    square = (heads, width, width)
    unit = 2 * tokens * tokens * width * heads
    ring = lax.axis_size(CTX)
    members = lax.axis_size(HEADS)
    token_buffer = pltpu.VMEM(query.shape, bf16)
    flat_buffer = pltpu.VMEM(flat, f32)

    def sems(n):
        return pltpu.SemaphoreType.DMA((n,))

    def onward(x):
        return lax.ppermute(x, CTX, [(i, i + 1) for i in range(ring - 1)])

    have = jnp.minimum(lax.axis_index(CTX), WINDOW_BLOCKS - 1).astype(jnp.int32).reshape(1)
    key, value, have = tied(key, value, have)

    (kh,) = call(head_major_kernel, [shape(head_major, bf16)], [key], [flat_buffer])
    vh, states = call(
        state_kernel,
        [shape(head_major, bf16), shape(square, bf16)],
        [kh, value],
        [flat_buffer],
        unit // 4,
    )
    states, query, cotangent = tied(states, query, cotangent)
    pieces, kh, vh = tied(spread(states), kh, vh)
    total, kv0 = call(
        total_kernel,
        [shape(square[1:], bf16), shape((2, tokens, width), bf16)],
        [pieces, key2[:, 0], softmax_values[:, 0]],
    )
    total, kh, vh = tied(total, kh, vh)
    kv1 = onward(kv0)
    totals = [from_row(total, d, False) for d in (1, 3, 2)]
    qh, gh, loc = call(
        local_kernel,
        [shape(head_major, bf16), shape(head_major, f32), shape(head_major, f32)],
        [query, cotangent, gain, kh, vh],
        [flat_buffer, flat_buffer],
        2 * unit,
    )
    *totals, kv1, loc = tied(*totals, kv1, loc)
    prefix, kv1 = tied(spread(scanned(pieces, totals, False)), kv1)
    kv2 = onward(kv1)
    att, part = call(
        attention_kernel,
        [shape(head_major, f32), shape((members, 2, tokens), f32)],
        [loc, qh, gh, prefix],
        (),
        unit // 4,
    )
    gathered = lax.all_to_all(part, HEADS, 0, 0, tiled=True)
    gathered, kv2 = tied(gathered, kv2)
    da, block_grad, inverse = call(
        backward_kernel,
        [shape(head_major, bf16), shape(square, bf16), shape((tokens, width), f32)],
        [gathered, att, gh, qh],
        (),
        unit // 4,
    )
    back_pieces, att, da, inverse, kv2 = tied(spread(block_grad), att, da, inverse, kv2)
    kv3 = onward(kv2)
    back_total = row_total(back_pieces)
    back_near = from_row(back_total, 1, True)
    gq, normed, sq = call(
        query_gradient_kernel,
        [shape(query.shape, bf16), shape(query.shape, bf16), shape(flat, bf16)],
        [kh, vh, da, prefix, att, inverse, gain, query2],
        [flat_buffer, flat_buffer],
        2 * unit,
    )
    back_near, gq, da = tied(back_near, gq, da)
    back_far = from_row(pair_total(back_total, back_near), 2, True)
    pk, pv = call(
        key_value_local_kernel, [shape(head_major, bf16)] * 2, [qh, kh, vh, da], (), 4 * unit
    )
    back_far, pk, sq, kv3 = tied(back_far, pk, sq, kv3)
    suffix, sq = tied(spread(scanned(back_pieces, [back_near, back_far], True)), sq)
    normed, gq, gk, gv, attended = call(
        final_kernel,
        [shape(query.shape, bf16)] * 5,
        [have, sq, kv0, kv1, kv2, kv3, kh, vh, pk, pv, suffix, gq, normed],
        [
            token_buffer,
            pltpu.VMEM((2, WINDOW_BLOCKS, tokens, tokens), f32),
            flat_buffer,
            flat_buffer,
            token_buffer,
            token_buffer,
            sems(8),
            sems(2),
            pltpu.SemaphoreType.DMA((4, 2)),
        ],
        9 * unit,
        smem_first=True,
        vmem=32,
        hbm_out=range(5),
    )
    return normed, gq, gk, gv, attended


def solution(mesh):
    sizes = (4, 8, 4, 2)
    fine = Mesh(mesh.devices.reshape(sizes), ("y", "z", "x", "core"))
    tokens = P(CTX, HEADS, None)
    return jax.shard_map(
        local,
        mesh=fine,
        in_specs=(tokens, tokens, tokens, P(HEADS, None), tokens, tokens, tokens, tokens),
        out_specs=(tokens,) * 5,
        check_vma=False,
    )
```
